256 devices in a mesh: seq: 64 (over y, z_lo, x), fsdp: 4 (over z_hi, core).
Axes of the slice: x: 4, y: 4, z: 8 (z_hi: 2, z_lo: 4; z = z_hi * 4 + z_lo), core: 2. Of those that a mesh axis runs over, the one named last changes fastest.
Arguments:
- queries: bfloat16 [4, 128, 256, 1152], P('fsdp', 'seq'), may hold values from -36 to 36
- keys: bfloat16 [4, 128, 256, 1152], P('fsdp', 'seq'), may hold values from -5 to 5
- values: bfloat16 [4, 128, 256, 1152], P('fsdp', 'seq'), may hold values from -6 to 6
- cotangent: bfloat16 [4, 128, 256, 1152], P('fsdp', 'seq'), may hold values from -16 to 16
- out_weight: bfloat16 [1152, 1152], P('fsdp'), may hold values from -0.1875 to 0.1875
Outputs:
- output: bfloat16 [4, 128, 256, 1152], P('fsdp', 'seq')
- query_grad: bfloat16 [4, 128, 256, 1152], P('fsdp', 'seq')
- key_grad: bfloat16 [4, 128, 256, 1152], P('fsdp', 'seq')
- value_grad: bfloat16 [4, 128, 256, 1152], P('fsdp', 'seq')
- weight_grad: float32 [1152, 1152], P('fsdp', 'seq')
The draws below stay inside these ranges and needn't reach their ends.
All inputs are finite; a program needn't handle non-finite values.
Results may differ from the reference program's by a relative error of at most 0.0058.
Values may be sent and summed in bfloat16 or wider, within the bound.
No kernel may reach another device: no remote copies, remote signals or barrier semaphores. Data moves between devices by JAX's collectives and lax.ppermute only.
A program may use at most 128 MiB of HBM per device.

```python
import jax
import jax.numpy as jnp
from jax import lax

D = 1152
HEADS = 16
HEAD_DIM = 72
PATCHES = 256
FRAMES = 128
CLIPS = 4


def draw_queries(key, part):
    key = jax.random.fold_in(key, 11)
    drawn = jax.random.normal(key, (CLIPS, FRAMES, PATCHES, D), jnp.float32)
    return jnp.clip(drawn, -4.0, 4.0).astype(jnp.bfloat16)


def draw_keys(key, part):
    key = jax.random.fold_in(key, 23)
    drawn = jax.random.normal(key, (CLIPS, FRAMES, PATCHES, D), jnp.float32)
    return jnp.clip(drawn, -4.0, 4.0).astype(jnp.bfloat16)


def with_spikes(values, own_key, source, target, shards_of, factor):
    owner, partner = [(jnp.arange(values.shape[axis_at]) // (values.shape[axis_at] // shards_of)).reshape([-1 if axis == axis_at else 1 for axis in range(values.ndim)]) for axis_at in (source, target)]
    chosen = jax.random.permutation(own_key, shards_of)[partner]
    strong = (owner == chosen) | (owner == (partner + shards_of // 2) % shards_of)
    return jnp.where(strong, factor * values, values)


def level_of(stream_key, extent, cuts, smallest, largest):
    def one(dim, blocks):
        draws = jax.random.uniform(jax.random.fold_in(jax.random.fold_in(stream_key, 6), dim), (blocks,), jnp.float32, smallest / len(cuts), largest / len(cuts))
        return jnp.repeat(jnp.exp(draws), extent[dim] // blocks).reshape((-1,) + (1,) * (len(extent) - dim - 1))

    gain = one(*cuts[0])
    for cut in cuts[1:]:
        gain = gain * one(*cut)
    return gain


def normal_values(stream_key, dims, width, reach, shards=(), kind=jnp.bfloat16):
    values = jax.random.normal(stream_key, dims, jnp.float32) * width
    if len(shards) > 0:
        values = level_of(stream_key, dims, shards, -0.22, 0.18) * values
    return jnp.clip(values, min=-reach, max=reach).astype(kind)


def bell_draw_with(own_key, extent, scale, reach, split, heavy, held_as=jnp.bfloat16):
    values = scale * jax.random.normal(own_key, extent, jnp.float32)
    if split:
        values = values * level_of(own_key, extent, split, -0.22, 0.18)
    return jnp.clip(with_spikes(values, jax.random.fold_in(own_key, 3), *heavy), -reach, reach).astype(held_as)


def setup_inputs(seed: int = 0) -> dict:
    key_of = jax.random.split(jax.random.key(seed), 6)
    queries = draw_queries(jax.random.fold_in(key_of[5], 71), 0)
    keys = draw_keys(jax.random.fold_in(key_of[5], 71), 0)
    values = normal_values(key_of[2], (CLIPS, FRAMES, PATCHES, D), 1.0, 6.0, ((0, 4), (1, 64)))
    cotangent = bell_draw_with(key_of[3], (CLIPS, FRAMES, PATCHES, D), 1.0, 16.0, ((0, 4), (1, 64)), (1, 3, 64, 4.0))
    out_weight = normal_values(key_of[4], (D, D), D ** -0.5, 0.1875, ((0, 4),))
    return {"queries": queries, "keys": keys, "values": values, "cotangent": cotangent, "out_weight": out_weight}


def temporal_clip(queries, keys, values, cotangent, out_weight):
    frames, patches, features = queries.shape
    factor = HEAD_DIM ** -0.5

    def heads_view(tensor):
        return tensor.astype(jnp.float32).reshape(frames, patches, HEADS, HEAD_DIM)

    query_heads = heads_view(queries)
    key_heads = heads_view(keys)
    value_heads = heads_view(values)
    scores = jnp.einsum("fphd,ephd->phfe", query_heads, key_heads) * factor
    row_max = jnp.max(scores, axis=-1, keepdims=True)
    raised = jnp.exp(scores - row_max)
    probability = raised / jnp.sum(raised, axis=-1, keepdims=True)
    prob_low = probability.astype(jnp.bfloat16)
    prob_back = lax.optimization_barrier(prob_low).astype(jnp.float32)
    attended = jnp.einsum("phfe,ephd->fphd", prob_back, value_heads).astype(jnp.bfloat16)
    flat_att = attended.reshape(frames * patches, features)
    flat_cot = cotangent.reshape(frames * patches, features)
    output = jnp.dot(flat_att, out_weight, preferred_element_type=jnp.float32).astype(jnp.bfloat16)
    upstream = jnp.dot(flat_cot, out_weight.T, preferred_element_type=jnp.float32).astype(jnp.bfloat16)
    weight_grad = jnp.dot(flat_att.T, flat_cot, preferred_element_type=jnp.float32)
    up_heads = heads_view(upstream.reshape(frames, patches, features))
    value_grad = jnp.einsum("phfe,fphd->ephd", prob_back, up_heads).astype(jnp.bfloat16)
    prob_grad = jnp.einsum("fphd,ephd->phfe", up_heads, value_heads)
    centre = jnp.sum(probability * prob_grad, axis=-1, keepdims=True)
    score_grad = (probability * (prob_grad - centre) * factor).astype(jnp.bfloat16)
    score_back = lax.optimization_barrier(score_grad).astype(jnp.float32)
    query_grad = jnp.einsum("phfe,ephd->fphd", score_back, key_heads).astype(jnp.bfloat16)
    key_grad = jnp.einsum("phfe,fphd->ephd", score_back, query_heads).astype(jnp.bfloat16)
    shaped = (frames, patches, features)
    return (output.reshape(shaped), query_grad.reshape(shaped), key_grad.reshape(shaped),
            value_grad.reshape(shaped), weight_grad)


def reference(queries, keys, values, cotangent, out_weight):
    def one_clip(running, inputs):
        result = temporal_clip(inputs[0], inputs[1], inputs[2], inputs[3], out_weight)
        return running + result[4], (result[0], result[1], result[2], result[3])

    summed, outputs = lax.scan(one_clip, jnp.zeros((D, D), jnp.float32), (queries, keys, values, cotangent))
    return outputs[0], outputs[1], outputs[2], outputs[3], summed
```

```python
import functools

import jax
import jax.numpy as jnp
import numpy as np
from jax import lax
from jax.experimental import pallas as pl
from jax.experimental.pallas import tpu as pltpu
from jax.sharding import Mesh
from jax.sharding import PartitionSpec as P

HEADS = 16
HEAD_DIM = 72
D = 1152
SCALE = HEAD_DIM ** (-0.5)
LOG2E = 1.4426950408889634
CHUNKS = (1, 1, 1, 1)
VMEM = 48 * 1024 * 1024
F32 = jnp.float32
BF16 = jnp.bfloat16
SEQ = ("y", "zl", "x")
ROWS = ("zh", "c")


def order_to_slabs(np_):
    size = 128 * np_
    out = np.zeros((size, size), np.float32)
    for s in range(16):
        for a in range(4):
            for f in range(2):
                for p in range(np_):
                    out[((s * 4 + a) * 2 + f) * np_ + p, ((a * 2 + f) * 16 + s) * np_ + p] = 1
    return out


def order_to_patches(np_):
    size = 128 * np_
    out = np.zeros((size, size), np.float32)
    for s in range(16):
        for a in range(4):
            for f in range(2):
                for p in range(np_):
                    out[((a * np_ + p) * 16 + s) * 2 + f, ((s * 4 + a) * 2 + f) * np_ + p] = 1
    return out


def const(matrix):
    return jnp.asarray(matrix, BF16)


def move(order, rows):
    return jnp.dot(order, rows, preferred_element_type=F32).astype(BF16)


def whole(shape):
    return pl.BlockSpec(shape, lambda i: (0,) * len(shape))


def params():
    return pltpu.CompilerParams(vmem_limit_bytes=VMEM)


def pack_kernel(np_, order_ref, q_ref, k_ref, v_ref, c_ref, *out_refs):
    zl = lax.axis_index("zl")
    for k in range(4):
        start = pl.multiple_of((zl ^ k) * (16 * np_), 16)
        rows = [
            ref[0, f, pl.ds(start, 16 * np_), :]
            for ref in (q_ref, k_ref, v_ref, c_ref)
            for f in range(2)
        ]
        out_refs[k][...] = move(order_ref[...], jnp.concatenate(rows, axis=0))


def pack(np_, block, arrays):
    spec = pl.BlockSpec((1, 2, 64 * np_, D), lambda i: (0, 0, block, 0))
    size = 128 * np_
    return pl.pallas_call(
        functools.partial(pack_kernel, np_),
        grid=(1,),
        in_specs=[whole((size, size))] + [spec] * 4,
        out_specs=[whole((size, D))] * 4,
        out_shape=[jax.ShapeDtypeStruct((size, D), BF16)] * 4,
        compiler_params=params(),
        cost_estimate=pl.CostEstimate(
            flops=2 * 4 * size * size * D, bytes_accessed=16 * size * D, transcendentals=0
        ),
        name="pack",
    )(const(order_to_slabs(np_)), *arrays)


def attend_kernel(np_, order_ref, back_ref, r_ref, w_ref, s_ref, att_ref, cot_ref, x_ref, u_ref, y_ref):
    size = 128 * np_
    for b in range(4):
        t = move(order_ref[...], r_ref[pl.ds(b * size, size), :])
        for a in range(4):
            for p in range(np_):
                x_ref[a, pl.ds(p * 128 + b * 32, 32), :] = t[(a * np_ + p) * 32 : (a * np_ + p + 1) * 32]
    cot = x_ref[3]
    cot_ref[...] = cot
    u_ref[...] = lax.dot_general(
        cot, w_ref[...], (((1,), (1,)), ((), ())), preferred_element_type=F32
    ).astype(BF16)
    y_ref[...] = jnp.zeros_like(y_ref)
    lane = lax.broadcasted_iota(jnp.int32, (1, 256), 1)
    for j in range(8):
        first = (lane >= 16 * j) & (lane < 16 * j + 72)
        second = (lane >= 16 * j + 72) & (lane < 16 * j + 144)
        keep_first = first.astype(F32).astype(BF16)
        keep_second = second.astype(F32).astype(BF16)
        win = pl.ds(128 * j, 256)

        def both(t):
            return jnp.concatenate([t * keep_first, t * keep_second], axis=0)

        def split(t):
            return jnp.where(first, t[:128], jnp.where(second, t[128:], 0.0)).astype(BF16)

        for p in range(np_):
            rows = pl.ds(p * 128, 128)
            q = x_ref[0, rows, win]
            u = u_ref[rows, win]
            kk = both(x_ref[1, rows, win])
            vv = both(x_ref[2, rows, win])
            scores = lax.dot_general(kk, q, (((1,), (1,)), ((), ())), preferred_element_type=F32)
            scores = scores.reshape(2, 128, 128)
            top = jnp.max(scores, axis=1, keepdims=True)
            raised = jnp.exp2((scores - top) * (SCALE * LOG2E))
            prob = raised * (1.0 / jnp.sum(raised, axis=1, keepdims=True))
            low = prob.astype(BF16).reshape(256, 128)
            grad = lax.dot_general(vv, u, (((1,), (1,)), ((), ())), preferred_element_type=F32)
            grad = grad.reshape(2, 128, 128)
            centre = jnp.sum(prob * grad, axis=1, keepdims=True)
            sg = (prob * (grad - centre) * SCALE).astype(BF16).reshape(256, 128)
            y_ref[0, rows, win] += lax.dot_general(
                low, vv, (((0,), (0,)), ((), ())), preferred_element_type=F32
            ).astype(BF16)
            y_ref[1, rows, win] += lax.dot_general(
                sg, kk, (((0,), (0,)), ((), ())), preferred_element_type=F32
            ).astype(BF16)
            y_ref[2, rows, win] += split(jnp.dot(sg, q, preferred_element_type=F32))
            y_ref[3, rows, win] += split(jnp.dot(low, u, preferred_element_type=F32))
    att = y_ref[0]
    att_ref[...] = att
    y_ref[0] = jnp.dot(att, w_ref[...], preferred_element_type=F32).astype(BF16)
    for b in range(4):
        t = jnp.concatenate(
            [y_ref[a, pl.ds(p * 128 + b * 32, 32), :] for a in range(4) for p in range(np_)], axis=0
        )
        s_ref[pl.ds(b * size, size), :] = move(back_ref[...], t)


def attend(np_, received, weight):
    size = 128 * np_
    order = order_to_patches(np_)
    return pl.pallas_call(
        functools.partial(attend_kernel, np_),
        grid=(1,),
        in_specs=[whole((size, size))] * 2 + [whole((4 * size, D)), whole((D, D))],
        out_specs=[whole((4 * size, D)), whole((size, D)), whole((size, D))],
        out_shape=[
            jax.ShapeDtypeStruct((4 * size, D), BF16),
            jax.ShapeDtypeStruct((size, D), BF16),
            jax.ShapeDtypeStruct((size, D), BF16),
        ],
        scratch_shapes=[
            pltpu.VMEM((4, size, D), BF16),
            pltpu.VMEM((size, D), BF16),
            pltpu.VMEM((4, size, D), BF16),
        ],
        compiler_params=params(),
        cost_estimate=pl.CostEstimate(
            flops=6_000_000_000 * np_ // 2, bytes_accessed=20 * size * D + 2 * D * D, transcendentals=262144 * np_
        ),
        name="attend",
    )(const(order), const(order.T.copy()), received, weight)


def unpack_kernel(np_, first, *refs):
    order_ref = refs[0]
    slabs = refs[1:5]
    outs = refs[5:] if first else refs[9:]
    zl = lax.axis_index("zl")
    for k in range(4):
        start = pl.multiple_of((zl ^ k) * (16 * np_), 16)
        t = move(order_ref[...], slabs[k][...])
        for a in range(4):
            for f in range(2):
                at = (a * 2 + f) * 16 * np_
                outs[a][0, f, pl.ds(start, 16 * np_), :] = t[at : at + 16 * np_]


def unpack(np_, block, slabs, before):
    size = 128 * np_
    spec = pl.BlockSpec((1, 2, 64 * np_, D), lambda i: (0, 0, block, 0))
    first = before is None
    return pl.pallas_call(
        functools.partial(unpack_kernel, np_, first),
        grid=(1,),
        in_specs=[whole((size, size))]
        + [whole((size, D))] * 4
        + ([] if first else [pl.BlockSpec(memory_space=pl.ANY)] * 4),
        out_specs=[spec] * 4,
        out_shape=[jax.ShapeDtypeStruct((1, 2, 256, D), BF16)] * 4,
        input_output_aliases={} if first else {5 + a: a for a in range(4)},
        compiler_params=params(),
        cost_estimate=pl.CostEstimate(
            flops=2 * 4 * size * size * D, bytes_accessed=16 * size * D, transcendentals=0
        ),
        name="unpack",
    )(const(order_to_slabs(np_).T.copy()), *slabs, *([] if first else before))


def outer_kernel(n, *refs):
    atts, cots = refs[:n], refs[n : 2 * n]
    mine_ref, theirs_ref = refs[2 * n :]
    att = jnp.concatenate([r[...] for r in atts], axis=0)
    cot = jnp.concatenate([r[...] for r in cots], axis=0)
    parts = [att[:, 288 * b : 288 * b + 288] for b in range(4)]
    even = jnp.concatenate([parts[0], parts[2]], axis=1)
    odd = jnp.concatenate([parts[1], parts[3]], axis=1)
    core = lax.axis_index("c")

    def product(t):
        return lax.dot_general(cot, t, (((0,), (0,)), ((), ())), preferred_element_type=F32)

    mine_ref[...] = product(jnp.where(core == 0, even, odd))
    theirs_ref[...] = product(jnp.where(core == 0, odd, even)).astype(theirs_ref.dtype)


def outer(atts, cots):
    n = len(atts)
    return pl.pallas_call(
        functools.partial(outer_kernel, n),
        grid=(1,),
        in_specs=[whole(t.shape) for t in (*atts, *cots)],
        out_specs=[whole((D, 576))] * 2,
        out_shape=[jax.ShapeDtypeStruct((D, 576), F32), jax.ShapeDtypeStruct((D, 576), BF16)],
        compiler_params=params(),
        cost_estimate=pl.CostEstimate(
            flops=2 * 512 * D * D, bytes_accessed=4 * 512 * D + 6 * D * 576, transcendentals=0
        ),
        name="outer",
    )(*atts, *cots)


def halves_kernel(mine_ref, other_ref, own_ref, *out_refs):
    y = lax.axis_index("y")
    for k in range(4):
        rows = pl.ds(pl.multiple_of((y ^ k) * 288, 32), 288)
        total = mine_ref[rows, :] + other_ref[rows, :].astype(F32)
        if k == 0:
            own_ref[...] = total
        else:
            out_refs[k - 1][...] = total.astype(BF16)


def halves(mine, other):
    return pl.pallas_call(
        halves_kernel,
        grid=(1,),
        in_specs=[whole((D, 576))] * 2,
        out_specs=[whole((288, 576))] * 4,
        out_shape=[jax.ShapeDtypeStruct((288, 576), F32)] + [jax.ShapeDtypeStruct((288, 576), BF16)] * 3,
        compiler_params=params(),
        cost_estimate=pl.CostEstimate(flops=D * 576, bytes_accessed=10 * D * 576, transcendentals=0),
        name="halves",
    )(mine, other)


def swap(value, axis, k):
    size = 2 if axis in ("zh", "c") else 4
    return lax.ppermute(value, axis, [(i, i ^ k) for i in range(size)])


def sum_over(blocks, axis, size):
    at = lax.axis_index(axis)
    total = lax.dynamic_index_in_dim(blocks, at, 0, keepdims=False)
    for k in range(1, size):
        total = total + swap(lax.dynamic_index_in_dim(blocks, at ^ k, 0, keepdims=False), axis, k)
    return total


def weight_total(atts, cots):
    mine, theirs = outer(atts, cots)
    own, *sent = halves(mine, swap(theirs, "c", 1))
    total = own
    for k in range(1, 4):
        total = total + swap(sent[k - 1], "y", k).astype(F32)
    blocks = total.reshape(4, 4, 18, 576).transpose(1, 0, 2, 3)
    blocks = sum_over(blocks, "x", 4)
    blocks = sum_over(blocks, "zl", 4)
    blocks = blocks.reshape(18, 2, 288).transpose(1, 0, 2)
    return sum_over(blocks, "zh", 2).T


def on_device(queries, keys, values, cotangent, out_weight):
    x = lax.axis_index("x")
    piece = lax.dynamic_slice_in_dim(out_weight, x * 72, 72, 0)
    weight = lax.all_gather(piece, ("zh", "c", "x"), axis=0, tiled=True)
    arrays = (queries, keys, values, cotangent)
    starts = [sum(CHUNKS[:i]) for i in range(len(CHUNKS))]
    received = []
    for np_, start in zip(CHUNKS, starts):
        slabs = pack(np_, start // np_, arrays)
        slabs = [slabs[0]] + [swap(slabs[k], "zl", k) for k in range(1, 4)]
        stacked = jnp.stack([s.reshape(16, 8 * np_, D) for s in slabs], axis=1)
        stacked = stacked.reshape(16, 32 * np_, D)
        got = lax.all_to_all(stacked, ("y", "x"), split_axis=0, concat_axis=0, tiled=True)
        received.append(got.reshape(512 * np_, D))
    sent, atts, cots = [], [], []
    for np_, got in zip(CHUNKS, received):
        out, att, cot = attend(np_, got, weight)
        sent.append(out)
        atts.append(att)
        cots.append(cot)
    weight_grad = weight_total(atts, cots)
    done = None
    for np_, start, out in zip(CHUNKS, starts, sent):
        got = lax.all_to_all(
            out.reshape(16, 32 * np_, D), ("y", "x"), split_axis=0, concat_axis=0, tiled=True
        )
        got = got.reshape(16, 4, 8 * np_, D)
        slabs = [got[:, k].reshape(128 * np_, D) for k in range(4)]
        slabs = [slabs[0]] + [swap(slabs[k], "zl", k) for k in range(1, 4)]
        done = unpack(np_, start // np_, slabs, done)
    return (*done, weight_grad)


def solution(mesh):
    fine = Mesh(mesh.devices.reshape(4, 4, 4, 2, 2), ("y", "zl", "x", "zh", "c"))
    frames = P(ROWS, SEQ, None, None)
    return jax.shard_map(
        on_device,
        mesh=fine,
        in_specs=(frames, frames, frames, frames, P(ROWS, None)),
        out_specs=(frames, frames, frames, frames, P(ROWS, SEQ)),
        check_vma=False,
    )
```

```python
import functools

import jax
import jax.numpy as jnp
import numpy as np
from jax import lax
from jax.experimental import pallas as pl
from jax.experimental.pallas import tpu as pltpu
from jax.sharding import Mesh
from jax.sharding import PartitionSpec as P

HEADS = 16
HEAD_DIM = 72
D = 1152
SCALE = HEAD_DIM ** (-0.5)
LOG2E = 1.4426950408889634
MIB = 1024 * 1024
F32 = jnp.float32
BF16 = jnp.bfloat16
SEQ = ("y", "zl", "x")
ROWS = ("zh", "c")


def order_to_slabs(np_):
    size = 128 * np_
    out = np.zeros((size, size), np.float32)
    for s in range(16):
        for a in range(4):
            for f in range(2):
                for p in range(np_):
                    out[((s * 4 + a) * 2 + f) * np_ + p, ((a * 2 + f) * 16 + s) * np_ + p] = 1
    return out


def order_to_patches(np_):
    size = 128 * np_
    out = np.zeros((size, size), np.float32)
    for s in range(16):
        for a in range(4):
            for f in range(2):
                for p in range(np_):
                    out[((a * np_ + p) * 16 + s) * 2 + f, ((s * 4 + a) * 2 + f) * np_ + p] = 1
    return out


def const(matrix):
    return jnp.asarray(matrix, BF16)


def move(order, rows):
    return jnp.dot(order, rows, preferred_element_type=F32).astype(BF16)


def whole(shape):
    return pl.BlockSpec(shape, lambda i: (0,) * len(shape))


def params(mib):
    return pltpu.CompilerParams(vmem_limit_bytes=mib * MIB)


def in_vmem(count):
    return [pl.BlockSpec(memory_space=pltpu.VMEM)] * count


def pack_kernel(order_ref, q_ref, k_ref, v_ref, c_ref, out_ref):
    rows = [ref[0, f] for ref in (q_ref, k_ref, v_ref, c_ref) for f in range(2)]
    out_ref[...] = move(order_ref[...], jnp.concatenate(rows, axis=0)).reshape(16, 16, D)


def pack(arrays):
    return pl.pallas_call(
        pack_kernel,
        grid=(2, 4),
        in_specs=[pl.BlockSpec((256, 256), lambda i, g: (0, 0))]
        + [pl.BlockSpec((1, 2, 32, D), lambda i, g: (0, 0, 4 * i + g, 0))] * 4,
        out_specs=pl.BlockSpec((16, 16, D), lambda i, g: (g, i, 0)),
        out_shape=jax.ShapeDtypeStruct((64, 32, D), BF16),
        compiler_params=params(60),
        cost_estimate=pl.CostEstimate(
            flops=2 * 2048 * 256 * D, bytes_accessed=8192 * D, transcendentals=0
        ),
        name="pack",
    )(const(order_to_slabs(2)), *arrays)


def attend_part(part, order_ref, back_ref, r_ref, w_ref, s_ref, att_ref, cot_ref, x_ref, u_ref, y_ref):
    slots = pl.ds(pl.multiple_of(part * 16, 16), 16)
    mine = pl.ds(pl.multiple_of(part * 256, 256), 256)
    for b in range(4):
        t = r_ref[pl.ds(b * 16, 16), slots, :].reshape(256, D)
        t = move(order_ref[...], t)
        for a in range(4):
            for p in range(2):
                x_ref[a, pl.ds(p * 128 + b * 32, 32), :] = t[(a * 2 + p) * 32 : (a * 2 + p + 1) * 32]
    cot = x_ref[3]
    cot_ref[mine, :] = cot
    u_ref[...] = lax.dot_general(
        cot, w_ref[...], (((1,), (1,)), ((), ())), preferred_element_type=F32
    ).astype(BF16)
    y_ref[...] = jnp.zeros_like(y_ref)
    lane = lax.broadcasted_iota(jnp.int32, (1, 256), 1)
    for j in range(8):
        first = (lane >= 16 * j) & (lane < 16 * j + 72)
        second = (lane >= 16 * j + 72) & (lane < 16 * j + 144)
        keep_first = first.astype(F32).astype(BF16)
        keep_second = second.astype(F32).astype(BF16)
        win = pl.ds(128 * j, 256)

        def both(t):
            return jnp.concatenate([t * keep_first, t * keep_second], axis=0)

        def split(t):
            return jnp.where(first, t[:128], jnp.where(second, t[128:], 0.0)).astype(BF16)

        for p in range(2):
            rows = pl.ds(p * 128, 128)
            q = x_ref[0, rows, win]
            u = u_ref[rows, win]
            kk = both(x_ref[1, rows, win])
            vv = both(x_ref[2, rows, win])
            scores = lax.dot_general(kk, q, (((1,), (1,)), ((), ())), preferred_element_type=F32)
            scores = scores.reshape(2, 128, 128)
            top = jnp.max(scores, axis=1, keepdims=True)
            raised = jnp.exp2((scores - top) * (SCALE * LOG2E))
            prob = raised * (1.0 / jnp.sum(raised, axis=1, keepdims=True))
            low = prob.astype(BF16).reshape(256, 128)
            grad = lax.dot_general(vv, u, (((1,), (1,)), ((), ())), preferred_element_type=F32)
            grad = grad.reshape(2, 128, 128)
            centre = jnp.sum(prob * grad, axis=1, keepdims=True)
            sg = (prob * (grad - centre) * SCALE).astype(BF16).reshape(256, 128)
            y_ref[0, rows, win] += lax.dot_general(
                low, vv, (((0,), (0,)), ((), ())), preferred_element_type=F32
            ).astype(BF16)
            y_ref[1, rows, win] += lax.dot_general(
                sg, kk, (((0,), (0,)), ((), ())), preferred_element_type=F32
            ).astype(BF16)
            y_ref[2, rows, win] += split(jnp.dot(sg, q, preferred_element_type=F32))
            y_ref[3, rows, win] += split(jnp.dot(low, u, preferred_element_type=F32))
    att = y_ref[0]
    att_ref[mine, :] = att
    y_ref[0] = jnp.dot(att, w_ref[...], preferred_element_type=F32).astype(BF16)
    for b in range(4):
        t = jnp.concatenate(
            [y_ref[a, pl.ds(p * 128 + b * 32, 32), :] for a in range(4) for p in range(2)], axis=0
        )
        s_ref[pl.ds(b * 16, 16), slots, :] = move(back_ref[...], t).reshape(16, 16, D)


def attend_kernel(*refs):
    @pl.loop(0, 2)
    def _(part):
        attend_part(part, *refs)


def attend(received, weight):
    order = order_to_patches(2)
    return pl.pallas_call(
        attend_kernel,
        in_specs=in_vmem(4),
        out_specs=in_vmem(3),
        out_shape=[
            jax.ShapeDtypeStruct((64, 32, D), BF16),
            jax.ShapeDtypeStruct((512, D), BF16),
            jax.ShapeDtypeStruct((512, D), BF16),
        ],
        scratch_shapes=[
            pltpu.VMEM((4, 256, D), BF16),
            pltpu.VMEM((256, D), BF16),
            pltpu.VMEM((4, 256, D), BF16),
        ],
        compiler_params=params(24),
        cost_estimate=pl.CostEstimate(
            flops=12_000_000_000, bytes_accessed=40 * 256 * D + 2 * D * D, transcendentals=1048576
        ),
        name="attend",
    )(const(order), const(order.T.copy()), received, weight)


def unpack_kernel(order_ref, slabs_ref, *outs):
    t = move(order_ref[...], slabs_ref[...].reshape(256, D))
    for a in range(4):
        for f in range(2):
            at = (a * 2 + f) * 32
            outs[a][0, f] = t[at : at + 32]


def unpack(slabs):
    return pl.pallas_call(
        unpack_kernel,
        grid=(2, 4),
        in_specs=[
            pl.BlockSpec((256, 256), lambda i, g: (0, 0)),
            pl.BlockSpec((16, 16, D), lambda i, g: (g, i, 0)),
        ],
        out_specs=[pl.BlockSpec((1, 2, 32, D), lambda i, g: (0, 0, 4 * i + g, 0))] * 4,
        out_shape=[jax.ShapeDtypeStruct((1, 2, 256, D), BF16)] * 4,
        compiler_params=params(60),
        cost_estimate=pl.CostEstimate(
            flops=2 * 2048 * 256 * D, bytes_accessed=8192 * D, transcendentals=0
        ),
        name="unpack",
    )(const(order_to_slabs(2).T.copy()), slabs)


def outer_kernel(att_ref, cot_ref, mine_ref, theirs_ref):
    att = att_ref[...]
    cot = cot_ref[...]
    parts = [att[:, 288 * b : 288 * b + 288] for b in range(4)]
    even = jnp.concatenate([parts[0], parts[2]], axis=1)
    odd = jnp.concatenate([parts[1], parts[3]], axis=1)
    core = lax.axis_index("c")

    def product(t):
        return lax.dot_general(cot, t, (((0,), (0,)), ((), ())), preferred_element_type=F32)

    mine_ref[...] = product(jnp.where(core == 0, even, odd))
    theirs_ref[...] = product(jnp.where(core == 0, odd, even)).astype(theirs_ref.dtype)


def outer(att, cot):
    return pl.pallas_call(
        outer_kernel,
        in_specs=in_vmem(2),
        out_specs=in_vmem(2),
        out_shape=[jax.ShapeDtypeStruct((D, 576), F32), jax.ShapeDtypeStruct((D, 576), BF16)],
        compiler_params=params(24),
        cost_estimate=pl.CostEstimate(
            flops=2 * 512 * D * D, bytes_accessed=4 * 512 * D + 6 * D * 576, transcendentals=0
        ),
        name="outer",
    )(att, cot)


def halves_kernel(mine_ref, other_ref, own_ref, *out_refs):
    y = lax.axis_index("y")
    for k in range(4):
        rows = pl.ds(pl.multiple_of((y ^ k) * 288, 32), 288)
        total = mine_ref[rows, :] + other_ref[rows, :].astype(F32)
        if k == 0:
            own_ref[...] = total
        else:
            out_refs[k - 1][...] = total.astype(BF16)


def halves(mine, other):
    return pl.pallas_call(
        halves_kernel,
        in_specs=in_vmem(2),
        out_specs=in_vmem(4),
        out_shape=[jax.ShapeDtypeStruct((288, 576), F32)] + [jax.ShapeDtypeStruct((288, 576), BF16)] * 3,
        compiler_params=params(24),
        cost_estimate=pl.CostEstimate(flops=D * 576, bytes_accessed=10 * D * 576, transcendentals=0),
        name="halves",
    )(mine, other)


def swap(value, axis, k):
    size = 2 if axis in ("zh", "c") else 4
    return lax.ppermute(value, axis, [(i, i ^ k) for i in range(size)])


def sum_over(blocks, axis, size):
    at = lax.axis_index(axis)
    total = lax.dynamic_index_in_dim(blocks, at, 0, keepdims=False)
    for k in range(1, size):
        total = total + swap(lax.dynamic_index_in_dim(blocks, at ^ k, 0, keepdims=False), axis, k)
    return total


def weight_total(att, cot):
    mine, theirs = outer(att, cot)
    own, *sent = halves(mine, swap(theirs, "c", 1))
    total = own
    for k in range(1, 4):
        total = total + swap(sent[k - 1], "y", k).astype(F32)
    blocks = total.reshape(4, 4, 18, 576).transpose(1, 0, 2, 3)
    blocks = sum_over(blocks, "x", 4)
    blocks = sum_over(blocks, "zl", 4)
    blocks = blocks.reshape(18, 2, 288).transpose(1, 0, 2)
    return sum_over(blocks, "zh", 2).T


def by_rank(axis, own, other):
    first = lax.axis_index(axis) == 0
    return jnp.stack([jnp.where(first, own, other), jnp.where(first, other, own)])


def whole_weight(out_weight):
    place = lax.axis_index("y") * 4 + lax.axis_index("x")
    piece = lax.dynamic_index_in_dim(out_weight.reshape(16, 18, D), place, 0, keepdims=False)
    pair = by_rank("zh", piece, swap(piece, "zh", 1))
    rows = lax.all_gather(pair, ("y", "x"), axis=0, tiled=False)
    rows = rows.transpose(1, 0, 2, 3).reshape(2, 288, D)
    both = by_rank("c", rows, swap(rows, "c", 1))
    return both.transpose(1, 0, 2, 3).reshape(D, D)


def exchange(t):
    return lax.all_to_all(t, SEQ, split_axis=0, concat_axis=0, tiled=True)


def on_device(queries, keys, values, cotangent, out_weight):
    weight = whole_weight(out_weight)
    received = exchange(pack((queries, keys, values, cotangent)))
    sent, att, cot = attend(received, weight)
    weight_grad = weight_total(att, cot)
    return (*unpack(exchange(sent)), weight_grad)


def solution(mesh):
    fine = Mesh(mesh.devices.reshape(4, 4, 4, 2, 2), ("y", "zl", "x", "zh", "c"))
    frames = P(ROWS, SEQ, None, None)
    return jax.shard_map(
        on_device,
        mesh=fine,
        in_specs=(frames, frames, frames, frames, P(ROWS, None)),
        out_specs=(frames, frames, frames, frames, P(ROWS, SEQ)),
        check_vma=False,
    )
```

```python
import functools

import jax
import jax.numpy as jnp
import numpy as np
from jax import lax
from jax.experimental import pallas as pl
from jax.experimental.pallas import tpu as pltpu
from jax.sharding import Mesh
from jax.sharding import PartitionSpec as P

HEADS = 16
HEAD_DIM = 72
D = 1152
SCALE = HEAD_DIM ** (-0.5)
LOG2E = 1.4426950408889634
MIB = 1024 * 1024
F32 = jnp.float32
BF16 = jnp.bfloat16
SEQ = ("y", "zl", "x")
ROWS = ("zh", "c")


def order_to_slabs(np_):
    size = 128 * np_
    out = np.zeros((size, size), np.float32)
    for s in range(16):
        for a in range(4):
            for f in range(2):
                for p in range(np_):
                    out[((s * 4 + a) * 2 + f) * np_ + p, ((a * 2 + f) * 16 + s) * np_ + p] = 1
    return out


def order_to_patches(np_):
    size = 128 * np_
    out = np.zeros((size, size), np.float32)
    for s in range(16):
        for a in range(4):
            for f in range(2):
                for p in range(np_):
                    out[((a * np_ + p) * 16 + s) * 2 + f, ((s * 4 + a) * 2 + f) * np_ + p] = 1
    return out


def const(matrix):
    return jnp.asarray(matrix, BF16)


def move(order, rows):
    return jnp.dot(order, rows, preferred_element_type=F32).astype(BF16)


def whole(shape):
    return pl.BlockSpec(shape, lambda i: (0,) * len(shape))


def params(mib):
    return pltpu.CompilerParams(vmem_limit_bytes=mib * MIB)


def anywhere(count):
    return [pl.BlockSpec(memory_space=pl.ANY)] * count


def in_vmem(count):
    return [pl.BlockSpec(memory_space=pltpu.VMEM)] * count


def pack_kernel(part, order_ref, q_ref, k_ref, v_ref, c_ref, *refs):
    out_ref, rows_ref, slabs_ref, in_sem, out_sem = refs[-5:]
    arrays = (q_ref, k_ref, v_ref, c_ref)
    coming, going = [], []
    for a in range(4):
        coming.append(
            pltpu.make_async_copy(
                arrays[a].at[0, :, pl.ds(part * 128, 128), :], rows_ref.at[a], in_sem.at[a]
            )
        )
        coming[-1].start()
    for copy in coming:
        copy.wait()
    for g in range(4):
        rows = [rows_ref[a, f, pl.ds(g * 32, 32), :] for a in range(4) for f in range(2)]
        slabs_ref[g] = move(order_ref[...], jnp.concatenate(rows, axis=0)).reshape(16, 16, D)
        going.append(
            pltpu.make_async_copy(
                slabs_ref.at[g],
                out_ref.at[pl.ds(g * 16, 16), pl.ds(part * 16, 16), :],
                out_sem.at[g],
            )
        )
        going[-1].start()
    for copy in going:
        copy.wait()


def pack(part, arrays, before):
    return pl.pallas_call(
        functools.partial(pack_kernel, part),
        in_specs=in_vmem(1) + anywhere(4 + len(before)),
        out_specs=pl.BlockSpec(memory_space=pl.ANY),
        out_shape=jax.ShapeDtypeStruct((64, 32, D), BF16),
        scratch_shapes=[
            pltpu.VMEM((4, 2, 128, D), BF16),
            pltpu.VMEM((4, 16, 16, D), BF16),
            pltpu.SemaphoreType.DMA((4,)),
            pltpu.SemaphoreType.DMA((4,)),
        ],
        input_output_aliases={5: 0} if before else {},
        compiler_params=params(60),
        cost_estimate=pl.CostEstimate(
            flops=2 * 1024 * 256 * D, bytes_accessed=4096 * D, transcendentals=0
        ),
        name="pack",
    )(const(order_to_slabs(2)), *arrays, *before)


def attend_part(part, order_ref, back_ref, r_ref, w_ref, s_ref, att_ref, cot_ref, *refs):
    in_ref, x_ref, u_ref, y_ref, out_ref, kept_ref, in_sem, out_sem, kept_sem = refs
    slots = pl.ds(pl.multiple_of(part * 16, 16), 16)
    mine = pl.ds(pl.multiple_of(part * 256, 256), 256)
    for b in range(4):
        n = part * 4 + b
        pltpu.make_async_copy(r_ref.at[pl.ds(b * 16, 16), slots, :], in_ref.at[n], in_sem.at[n]).wait()
        t = move(order_ref[...], in_ref[n].reshape(256, D))
        for a in range(4):
            for p in range(2):
                x_ref[a, pl.ds(p * 128 + b * 32, 32), :] = t[(a * 2 + p) * 32 : (a * 2 + p + 1) * 32]
    cot = x_ref[3]
    kept_ref[part, 1] = cot
    pltpu.make_async_copy(kept_ref.at[part, 1], cot_ref.at[mine, :], kept_sem.at[part, 1]).start()
    u_ref[...] = lax.dot_general(
        cot, w_ref[...], (((1,), (1,)), ((), ())), preferred_element_type=F32
    ).astype(BF16)
    y_ref[...] = jnp.zeros_like(y_ref)
    lane = lax.broadcasted_iota(jnp.int32, (1, 256), 1)
    for j in range(8):
        first = (lane >= 16 * j) & (lane < 16 * j + 72)
        second = (lane >= 16 * j + 72) & (lane < 16 * j + 144)
        keep_first = first.astype(F32).astype(BF16)
        keep_second = second.astype(F32).astype(BF16)
        win = pl.ds(128 * j, 256)

        def both(t):
            return jnp.concatenate([t * keep_first, t * keep_second], axis=0)

        def beside(t):
            return jnp.concatenate([t[:128], t[128:]], axis=1)

        for p in range(2):
            rows = pl.ds(p * 128, 128)
            q = x_ref[0, rows, win]
            u = u_ref[rows, win]
            kk = both(x_ref[1, rows, win])
            vv = both(x_ref[2, rows, win])
            scores = lax.dot_general(kk, q, (((1,), (1,)), ((), ())), preferred_element_type=F32)
            scores = scores.reshape(2, 128, 128)
            top = jnp.max(scores, axis=1, keepdims=True)
            raised = jnp.exp2((scores - top) * (SCALE * LOG2E))
            prob = raised * (1.0 / jnp.sum(raised, axis=1, keepdims=True))
            low = prob.astype(BF16).reshape(256, 128)
            grad = lax.dot_general(vv, u, (((1,), (1,)), ((), ())), preferred_element_type=F32)
            grad = grad.reshape(2, 128, 128)
            centre = jnp.sum(prob * grad, axis=1, keepdims=True)
            sg = (prob * (grad - centre) * SCALE).astype(BF16).reshape(256, 128)
            y_ref[0, rows, win] += lax.dot_general(
                low, vv, (((0,), (0,)), ((), ())), preferred_element_type=F32
            ).astype(BF16)
            y_ref[1, rows, win] += lax.dot_general(
                sg, kk, (((0,), (0,)), ((), ())), preferred_element_type=F32
            ).astype(BF16)
            y_ref[2, rows, win] += jnp.dot(
                beside(sg), both(q), preferred_element_type=F32
            ).astype(BF16)
            y_ref[3, rows, win] += jnp.dot(
                beside(low), both(u), preferred_element_type=F32
            ).astype(BF16)
    att = y_ref[0]
    kept_ref[part, 0] = att
    pltpu.make_async_copy(kept_ref.at[part, 0], att_ref.at[mine, :], kept_sem.at[part, 0]).start()
    y_ref[0] = jnp.dot(att, w_ref[...], preferred_element_type=F32).astype(BF16)
    for b in range(4):
        n = part * 4 + b
        t = jnp.concatenate(
            [y_ref[a, pl.ds(p * 128 + b * 32, 32), :] for a in range(4) for p in range(2)], axis=0
        )
        out_ref[n] = move(back_ref[...], t).reshape(16, 16, D)
        pltpu.make_async_copy(out_ref.at[n], s_ref.at[pl.ds(b * 16, 16), slots, :], out_sem.at[n]).start()


def attend_kernel(*refs):
    r_ref, s_ref, att_ref, cot_ref = refs[2], refs[4], refs[5], refs[6]
    in_ref, out_ref, kept_ref, in_sem, out_sem, kept_sem = refs[7], *refs[11:]
    for n in range(8):
        part, b = divmod(n, 4)
        pltpu.make_async_copy(
            r_ref.at[pl.ds(b * 16, 16), pl.ds(part * 16, 16), :], in_ref.at[n], in_sem.at[n]
        ).start()

    @pl.loop(0, 2)
    def _(part):
        attend_part(part, *refs)

    for part in range(2):
        for i, ref in enumerate((att_ref, cot_ref)):
            pltpu.make_async_copy(
                kept_ref.at[part, i], ref.at[pl.ds(part * 256, 256), :], kept_sem.at[part, i]
            ).wait()
        for b in range(4):
            n = part * 4 + b
            pltpu.make_async_copy(
                out_ref.at[n], s_ref.at[pl.ds(b * 16, 16), pl.ds(part * 16, 16), :], out_sem.at[n]
            ).wait()


def attend(received, weight):
    order = order_to_patches(2)
    return pl.pallas_call(
        attend_kernel,
        in_specs=in_vmem(2) + anywhere(1) + in_vmem(1),
        out_specs=anywhere(3),
        out_shape=[
            jax.ShapeDtypeStruct((64, 32, D), BF16),
            jax.ShapeDtypeStruct((512, D), BF16),
            jax.ShapeDtypeStruct((512, D), BF16),
        ],
        scratch_shapes=[
            pltpu.VMEM((8, 16, 16, D), BF16),
            pltpu.VMEM((4, 256, D), BF16),
            pltpu.VMEM((256, D), BF16),
            pltpu.VMEM((4, 256, D), BF16),
            pltpu.VMEM((8, 16, 16, D), BF16),
            pltpu.VMEM((2, 2, 256, D), BF16),
            pltpu.SemaphoreType.DMA((8,)),
            pltpu.SemaphoreType.DMA((8,)),
            pltpu.SemaphoreType.DMA((2, 2)),
        ],
        compiler_params=params(40),
        cost_estimate=pl.CostEstimate(
            flops=12_000_000_000, bytes_accessed=40 * 256 * D + 2 * D * D, transcendentals=1048576
        ),
        name="attend",
    )(const(order), const(order.T.copy()), received, weight)


def unpack_kernel(order_ref, slabs_ref, *refs):
    outs = refs[:4]
    in_ref, rows_ref, in_sem, out_sem = refs[4:]
    coming, going = [], []
    for n in range(8):
        part, g = divmod(n, 4)
        coming.append(
            pltpu.make_async_copy(
                slabs_ref.at[pl.ds(g * 16, 16), pl.ds(part * 16, 16), :], in_ref.at[n], in_sem.at[n]
            )
        )
        coming[-1].start()
    for n in range(8):
        part, g = divmod(n, 4)
        coming[n].wait()
        t = move(order_ref[...], in_ref[n].reshape(256, D))
        for a in range(4):
            for f in range(2):
                at = (a * 2 + f) * 32
                rows_ref[part, a, f, pl.ds(g * 32, 32), :] = t[at : at + 32]
            if g % 2 == 1:
                begin = (g - 1) * 32
                going.append(
                    pltpu.make_async_copy(
                        rows_ref.at[part, a, :, pl.ds(begin, 64), :],
                        outs[a].at[0, :, pl.ds(part * 128 + begin, 64), :],
                        out_sem.at[n, a],
                    )
                )
                going[-1].start()
    for copy in going:
        copy.wait()


def unpack(slabs):
    return pl.pallas_call(
        unpack_kernel,
        in_specs=in_vmem(1) + anywhere(1),
        out_specs=anywhere(4),
        out_shape=[jax.ShapeDtypeStruct((1, 2, 256, D), BF16)] * 4,
        scratch_shapes=[
            pltpu.VMEM((8, 16, 16, D), BF16),
            pltpu.VMEM((2, 4, 2, 128, D), BF16),
            pltpu.SemaphoreType.DMA((8,)),
            pltpu.SemaphoreType.DMA((8, 4)),
        ],
        compiler_params=params(60),
        cost_estimate=pl.CostEstimate(
            flops=2 * 2048 * 256 * D, bytes_accessed=8192 * D, transcendentals=0
        ),
        name="unpack",
    )(const(order_to_slabs(2).T.copy()), slabs)


def outer_kernel(att_ref, cot_ref, mine_ref, theirs_ref):
    att = att_ref[...]
    cot = cot_ref[...]
    parts = [att[:, 288 * b : 288 * b + 288] for b in range(4)]
    even = jnp.concatenate([parts[0], parts[2]], axis=1)
    odd = jnp.concatenate([parts[1], parts[3]], axis=1)
    core = lax.axis_index("c")

    def product(t):
        return lax.dot_general(cot, t, (((0,), (0,)), ((), ())), preferred_element_type=F32)

    mine_ref[...] = product(jnp.where(core == 0, even, odd))
    theirs_ref[...] = product(jnp.where(core == 0, odd, even)).astype(theirs_ref.dtype)


def outer(att, cot):
    return pl.pallas_call(
        outer_kernel,
        in_specs=in_vmem(2),
        out_specs=in_vmem(2),
        out_shape=[jax.ShapeDtypeStruct((D, 576), F32), jax.ShapeDtypeStruct((D, 576), BF16)],
        compiler_params=params(24),
        cost_estimate=pl.CostEstimate(
            flops=2 * 512 * D * D, bytes_accessed=4 * 512 * D + 6 * D * 576, transcendentals=0
        ),
        name="outer",
    )(att, cot)


def halves_kernel(mine_ref, other_ref, own_ref, *out_refs):
    y = lax.axis_index("y")
    for k in range(4):
        rows = pl.ds(pl.multiple_of((y ^ k) * 288, 32), 288)
        total = mine_ref[rows, :] + other_ref[rows, :].astype(F32)
        if k == 0:
            own_ref[...] = total
        else:
            out_refs[k - 1][...] = total.astype(BF16)


def halves(mine, other):
    return pl.pallas_call(
        halves_kernel,
        in_specs=in_vmem(2),
        out_specs=in_vmem(4),
        out_shape=[jax.ShapeDtypeStruct((288, 576), F32)] + [jax.ShapeDtypeStruct((288, 576), BF16)] * 3,
        compiler_params=params(24),
        cost_estimate=pl.CostEstimate(flops=D * 576, bytes_accessed=10 * D * 576, transcendentals=0),
        name="halves",
    )(mine, other)


def swap(value, axis, k):
    size = 2 if axis in ("zh", "c") else 4
    return lax.ppermute(value, axis, [(i, i ^ k) for i in range(size)])


def sum_over(blocks, axis, size):
    at = lax.axis_index(axis)
    total = lax.dynamic_index_in_dim(blocks, at, 0, keepdims=False)
    for k in range(1, size):
        total = total + swap(lax.dynamic_index_in_dim(blocks, at ^ k, 0, keepdims=False), axis, k)
    return total


def weight_total(att, cot):
    mine, theirs = outer(att, cot)
    own, *sent = halves(mine, swap(theirs, "c", 1))
    total = own
    for k in range(1, 4):
        total = total + swap(sent[k - 1], "y", k).astype(F32)
    blocks = total.reshape(4, 4, 18, 576).transpose(1, 0, 2, 3)
    blocks = sum_over(blocks, "x", 4)
    blocks = sum_over(blocks, "zl", 4)
    blocks = blocks.reshape(18, 2, 288).transpose(1, 0, 2)
    return sum_over(blocks, "zh", 2).T


def by_rank(axis, own, other):
    first = lax.axis_index(axis) == 0
    return jnp.stack([jnp.where(first, own, other), jnp.where(first, other, own)])


def weight_piece(out_weight):
    place = lax.axis_index("y") * 4 + lax.axis_index("x")
    piece = lax.dynamic_slice_in_dim(out_weight, place * 18, 18, 0)
    return by_rank("zh", piece, swap(piece, "zh", 1))


def whole_weight(pair):
    rows = lax.all_gather(pair, ("y", "x"), axis=0, tiled=False)
    rows = rows.transpose(1, 0, 2, 3).reshape(2, 288, D)
    both = by_rank("c", rows, swap(rows, "c", 1))
    return both.transpose(1, 0, 2, 3).reshape(D, D)


def exchange(t):
    return lax.all_to_all(t, SEQ, split_axis=0, concat_axis=0, tiled=True)


def on_device(queries, keys, values, cotangent, out_weight):
    arrays = (queries, keys, values, cotangent)
    pair = weight_piece(out_weight)
    packed = pack(0, arrays, ())
    packed = pack(1, arrays, (packed, pair))
    received = exchange(packed)
    sent, att, cot = attend(received, whole_weight(pair))
    weight_grad = weight_total(att, cot)
    return (*unpack(exchange(sent)), weight_grad)


def solution(mesh):
    fine = Mesh(mesh.devices.reshape(4, 4, 4, 2, 2), ("y", "zl", "x", "zh", "c"))
    frames = P(ROWS, SEQ, None, None)
    return jax.shard_map(
        on_device,
        mesh=fine,
        in_specs=(frames, frames, frames, frames, P(ROWS, None)),
        out_specs=(frames, frames, frames, frames, P(ROWS, SEQ)),
        check_vma=False,
    )
```

```python
import functools

import jax
import jax.numpy as jnp
import numpy as np
from jax import lax
from jax.experimental import pallas as pl
from jax.experimental.pallas import tpu as pltpu
from jax.sharding import Mesh
from jax.sharding import PartitionSpec as P

HEADS = 16
HEAD_DIM = 72
D = 1152
SCALE = HEAD_DIM ** (-0.5)
LOG2E = 1.4426950408889634
MIB = 1024 * 1024
F32 = jnp.float32
BF16 = jnp.bfloat16
SEQ = ("y", "zl", "x")
ROWS = ("zh", "c")


def order_to_slabs(np_):
    size = 128 * np_
    out = np.zeros((size, size), np.float32)
    for s in range(16):
        for a in range(4):
            for f in range(2):
                for p in range(np_):
                    out[((s * 4 + a) * 2 + f) * np_ + p, ((a * 2 + f) * 16 + s) * np_ + p] = 1
    return out


def order_to_patches(np_):
    size = 128 * np_
    out = np.zeros((size, size), np.float32)
    for s in range(16):
        for a in range(4):
            for f in range(2):
                for p in range(np_):
                    out[((a * np_ + p) * 16 + s) * 2 + f, ((s * 4 + a) * 2 + f) * np_ + p] = 1
    return out


def const(matrix):
    return jnp.asarray(matrix, BF16)


def move(order, rows):
    return jnp.dot(order, rows, preferred_element_type=F32).astype(BF16)


def whole(shape):
    return pl.BlockSpec(shape, lambda i: (0,) * len(shape))


def params(mib):
    return pltpu.CompilerParams(vmem_limit_bytes=mib * MIB)


def in_hbm(count):
    return [pl.BlockSpec(memory_space=pltpu.HBM)] * count


def in_vmem(count):
    return [pl.BlockSpec(memory_space=pltpu.VMEM)] * count


def pack_kernel(order_ref, q_ref, k_ref, v_ref, c_ref, out_ref, rows_ref, slabs_ref, in_sem, out_sem):
    arrays = (q_ref, k_ref, v_ref, c_ref)
    coming, going = [], []
    for part in range(2):
        for a in range(4):
            coming.append(
                pltpu.make_async_copy(
                    arrays[a].at[0, :, pl.ds(part * 128, 128), :],
                    rows_ref.at[part, a],
                    in_sem.at[part, a],
                )
            )
            coming[-1].start()
    for part in range(2):
        for a in range(4):
            coming[4 * part + a].wait()
        for g in range(4):
            rows = [rows_ref[part, a, f, pl.ds(g * 32, 32), :] for a in range(4) for f in range(2)]
            slabs_ref[part, g] = move(order_ref[...], jnp.concatenate(rows, axis=0)).reshape(16, 16, D)
            going.append(
                pltpu.make_async_copy(
                    slabs_ref.at[part, g],
                    out_ref.at[pl.ds(g * 16, 16), pl.ds(part * 16, 16), :],
                    out_sem.at[part, g],
                )
            )
            going[-1].start()
    for copy in going:
        copy.wait()


def pack(arrays):
    return pl.pallas_call(
        pack_kernel,
        in_specs=in_vmem(1) + in_hbm(4),
        out_specs=pl.BlockSpec(memory_space=pltpu.HBM),
        out_shape=jax.ShapeDtypeStruct((64, 32, D), BF16),
        scratch_shapes=[
            pltpu.VMEM((2, 4, 2, 128, D), BF16),
            pltpu.VMEM((2, 4, 16, 16, D), BF16),
            pltpu.SemaphoreType.DMA((2, 4)),
            pltpu.SemaphoreType.DMA((2, 4)),
        ],
        compiler_params=params(60),
        cost_estimate=pl.CostEstimate(
            flops=2 * 2048 * 256 * D, bytes_accessed=8192 * D, transcendentals=0
        ),
        name="pack",
    )(const(order_to_slabs(2)), *arrays)


def masks(j):
    lane = lax.broadcasted_iota(jnp.int32, (1, 256), 1)
    first = (lane >= 16 * j) & (lane < 16 * j + 72)
    second = (lane >= 16 * j + 72) & (lane < 16 * j + 144)
    return first.astype(F32).astype(BF16), second.astype(F32).astype(BF16)


def both(t, pair):
    return jnp.concatenate([t * pair[0], t * pair[1]], axis=0)


def beside(t):
    return jnp.concatenate([t[:128], t[128:]], axis=1)


def by_last(left, right):
    return lax.dot_general(left, right, (((1,), (1,)), ((), ())), preferred_element_type=F32)


def by_first(left, right):
    return lax.dot_general(left, right, (((0,), (0,)), ((), ())), preferred_element_type=F32)


def forward_part(part, order_ref, r_ref, x_hbm, in_ref, x_ref, att_ref, stat_ref, in_sem, x_sem):
    slots = pl.ds(pl.multiple_of(part * 16, 16), 16)
    for b in range(4):
        n = part * 4 + b
        pltpu.make_async_copy(r_ref.at[pl.ds(b * 16, 16), slots, :], in_ref.at[n], in_sem.at[n]).wait()
        t = move(order_ref[...], in_ref[n].reshape(256, D))
        for a in range(4):
            for p in range(2):
                x_ref[part, a, pl.ds(p * 128 + b * 32, 32), :] = t[(a * 2 + p) * 32 : (a * 2 + p + 1) * 32]
    pltpu.make_async_copy(x_ref.at[part], x_hbm.at[part], x_sem.at[part]).start()
    att_ref[part] = jnp.zeros((256, D), BF16)
    for j in range(8):
        pair = masks(j)
        win = pl.ds(128 * j, 256)
        for p in range(2):
            rows = pl.ds(p * 128, 128)
            kk = both(x_ref[part, 1, rows, win], pair)
            vv = both(x_ref[part, 2, rows, win], pair)
            scores = by_last(kk, x_ref[part, 0, rows, win]).reshape(2, 128, 128)
            top = jnp.max(scores, axis=1, keepdims=True)
            raised = jnp.exp2((scores - top) * (SCALE * LOG2E))
            scale = 1.0 / jnp.sum(raised, axis=1, keepdims=True)
            low = (raised * scale).astype(BF16).reshape(256, 128)
            att_ref[part, rows, win] += by_first(low, vv).astype(BF16)
            stat_ref[part, 2 * j + p, pl.ds(0, 2), :] = top.reshape(2, 128)
            stat_ref[part, 2 * j + p, pl.ds(2, 2), :] = scale.reshape(2, 128)


def forward_kernel(
    order_ref, r_ref, x_hbm, att_hbm, stat_hbm, mine_hbm, theirs_hbm,
    in_ref, x_ref, att_ref, stat_ref, mine_ref, theirs_ref, in_sem, x_sem, end_sem,
):
    for n in range(8):
        part, b = divmod(n, 4)
        pltpu.make_async_copy(
            r_ref.at[pl.ds(b * 16, 16), pl.ds(part * 16, 16), :], in_ref.at[n], in_sem.at[n]
        ).start()

    @pl.loop(0, 2)
    def _(part):
        forward_part(part, order_ref, r_ref, x_hbm, in_ref, x_ref, att_ref, stat_ref, in_sem, x_sem)

    ending = [
        pltpu.make_async_copy(att_ref, att_hbm, end_sem.at[0]),
        pltpu.make_async_copy(stat_ref, stat_hbm, end_sem.at[1]),
        pltpu.make_async_copy(theirs_ref, theirs_hbm, end_sem.at[2]),
        pltpu.make_async_copy(mine_ref, mine_hbm, end_sem.at[3]),
    ]
    ending[0].start()
    ending[1].start()
    att = jnp.concatenate([att_ref[0], att_ref[1]], axis=0)
    cot = jnp.concatenate([x_ref[0, 3], x_ref[1, 3]], axis=0)
    parts = [att[:, 288 * b : 288 * b + 288] for b in range(4)]
    even = jnp.concatenate([parts[0], parts[2]], axis=1)
    odd = jnp.concatenate([parts[1], parts[3]], axis=1)
    core = lax.axis_index("c")
    theirs_ref[...] = by_first(cot, jnp.where(core == 0, odd, even)).astype(BF16)
    ending[2].start()
    mine_ref[...] = by_first(cot, jnp.where(core == 0, even, odd))
    ending[3].start()
    for part in range(2):
        pltpu.make_async_copy(x_ref.at[part], x_hbm.at[part], x_sem.at[part]).wait()
    for copy in ending:
        copy.wait()


def forward(received):
    return pl.pallas_call(
        forward_kernel,
        in_specs=in_vmem(1) + in_hbm(1),
        out_specs=in_hbm(5),
        out_shape=[
            jax.ShapeDtypeStruct((2, 4, 256, D), BF16),
            jax.ShapeDtypeStruct((2, 256, D), BF16),
            jax.ShapeDtypeStruct((2, 16, 4, 128), F32),
            jax.ShapeDtypeStruct((D, 576), F32),
            jax.ShapeDtypeStruct((D, 576), BF16),
        ],
        scratch_shapes=[
            pltpu.VMEM((8, 16, 16, D), BF16),
            pltpu.VMEM((2, 4, 256, D), BF16),
            pltpu.VMEM((2, 256, D), BF16),
            pltpu.VMEM((2, 16, 4, 128), F32),
            pltpu.VMEM((D, 576), F32),
            pltpu.VMEM((D, 576), BF16),
            pltpu.SemaphoreType.DMA((8,)),
            pltpu.SemaphoreType.DMA((2,)),
            pltpu.SemaphoreType.DMA((4,)),
        ],
        compiler_params=params(58),
        cost_estimate=pl.CostEstimate(
            flops=5_000_000_000, bytes_accessed=40 * 256 * D, transcendentals=1048576
        ),
        name="forward",
    )(const(order_to_patches(2)), received)


def backward_part(part, back_ref, x_hbm, s_ref, x_ref, w_ref, att_ref, stat_ref, u_ref, y_ref, out_ref, x_sem, out_sem):
    slots = pl.ds(pl.multiple_of(part * 16, 16), 16)
    pltpu.make_async_copy(x_hbm.at[part], x_ref.at[part], x_sem.at[part]).wait()
    u_ref[...] = by_last(x_ref[part, 3], w_ref[...]).astype(BF16)
    y_ref[...] = jnp.zeros_like(y_ref)
    for j in range(8):
        pair = masks(j)
        win = pl.ds(128 * j, 256)
        for p in range(2):
            rows = pl.ds(p * 128, 128)
            q = x_ref[part, 0, rows, win]
            u = u_ref[rows, win]
            kk = both(x_ref[part, 1, rows, win], pair)
            vv = both(x_ref[part, 2, rows, win], pair)
            top = stat_ref[part, 2 * j + p, pl.ds(0, 2), :].reshape(2, 1, 128)
            scale = stat_ref[part, 2 * j + p, pl.ds(2, 2), :].reshape(2, 1, 128)
            scores = by_last(kk, q).reshape(2, 128, 128)
            prob = jnp.exp2((scores - top) * (SCALE * LOG2E)) * scale
            low = prob.astype(BF16).reshape(256, 128)
            grad = by_last(vv, u).reshape(2, 128, 128)
            centre = jnp.sum(prob * grad, axis=1, keepdims=True)
            sg = (prob * (grad - centre) * SCALE).astype(BF16).reshape(256, 128)
            y_ref[1, rows, win] += by_first(sg, kk).astype(BF16)
            y_ref[2, rows, win] += jnp.dot(
                beside(sg), both(q, pair), preferred_element_type=F32
            ).astype(BF16)
            y_ref[3, rows, win] += jnp.dot(
                beside(low), both(u, pair), preferred_element_type=F32
            ).astype(BF16)
    y_ref[0] = jnp.dot(att_ref[part], w_ref[...], preferred_element_type=F32).astype(BF16)
    for b in range(4):
        n = part * 4 + b
        t = jnp.concatenate(
            [y_ref[a, pl.ds(p * 128 + b * 32, 32), :] for a in range(4) for p in range(2)], axis=0
        )
        out_ref[n] = move(back_ref[...], t).reshape(16, 16, D)
        pltpu.make_async_copy(out_ref.at[n], s_ref.at[pl.ds(b * 16, 16), slots, :], out_sem.at[n]).start()


def backward_kernel(
    back_ref, x_hbm, att_hbm, stat_hbm, w_hbm, s_ref,
    x_ref, w_ref, att_ref, stat_ref, u_ref, y_ref, out_ref, x_sem, w_sem, in_sem, out_sem,
):
    coming = [pltpu.make_async_copy(stat_hbm, stat_ref, in_sem.at[0])]
    coming += [
        pltpu.make_async_copy(w_hbm.at[pl.ds(288 * b, 288), :], w_ref.at[pl.ds(288 * b, 288), :], w_sem.at[b])
        for b in range(4)
    ]
    coming.append(pltpu.make_async_copy(att_hbm, att_ref, in_sem.at[1]))
    pltpu.make_async_copy(x_hbm.at[0], x_ref.at[0], x_sem.at[0]).start()
    for copy in coming:
        copy.start()
    pltpu.make_async_copy(x_hbm.at[1], x_ref.at[1], x_sem.at[1]).start()
    for copy in coming:
        copy.wait()

    @pl.loop(0, 2)
    def _(part):
        backward_part(
            part, back_ref, x_hbm, s_ref, x_ref, w_ref, att_ref, stat_ref, u_ref, y_ref, out_ref, x_sem, out_sem
        )

    for n in range(8):
        part, b = divmod(n, 4)
        pltpu.make_async_copy(
            out_ref.at[n], s_ref.at[pl.ds(b * 16, 16), pl.ds(part * 16, 16), :], out_sem.at[n]
        ).wait()


def backward(arrays, att, stats, weight):
    return pl.pallas_call(
        backward_kernel,
        in_specs=in_vmem(1) + in_hbm(4),
        out_specs=pl.BlockSpec(memory_space=pltpu.HBM),
        out_shape=jax.ShapeDtypeStruct((64, 32, D), BF16),
        scratch_shapes=[
            pltpu.VMEM((2, 4, 256, D), BF16),
            pltpu.VMEM((D, D), BF16),
            pltpu.VMEM((2, 256, D), BF16),
            pltpu.VMEM((2, 16, 4, 128), F32),
            pltpu.VMEM((256, D), BF16),
            pltpu.VMEM((4, 256, D), BF16),
            pltpu.VMEM((8, 16, 16, D), BF16),
            pltpu.SemaphoreType.DMA((2,)),
            pltpu.SemaphoreType.DMA((4,)),
            pltpu.SemaphoreType.DMA((2,)),
            pltpu.SemaphoreType.DMA((8,)),
        ],
        compiler_params=params(58),
        cost_estimate=pl.CostEstimate(
            flops=9_000_000_000, bytes_accessed=40 * 256 * D + 2 * D * D, transcendentals=1048576
        ),
        name="backward",
    )(const(order_to_patches(2).T.copy()), arrays, att, stats, weight)


def unpack_kernel(order_ref, slabs_ref, *refs):
    outs = refs[:4]
    in_ref, rows_ref, in_sem, out_sem = refs[4:]
    coming, going = [], []
    for n in range(8):
        part, g = divmod(n, 4)
        coming.append(
            pltpu.make_async_copy(
                slabs_ref.at[pl.ds(g * 16, 16), pl.ds(part * 16, 16), :], in_ref.at[n], in_sem.at[n]
            )
        )
        coming[-1].start()
    for n in range(8):
        part, g = divmod(n, 4)
        coming[n].wait()
        t = move(order_ref[...], in_ref[n].reshape(256, D))
        for a in range(4):
            for f in range(2):
                at = (a * 2 + f) * 32
                rows_ref[part, a, f, pl.ds(g * 32, 32), :] = t[at : at + 32]
            if g % 2 == 1:
                begin = (g - 1) * 32
                going.append(
                    pltpu.make_async_copy(
                        rows_ref.at[part, a, :, pl.ds(begin, 64), :],
                        outs[a].at[0, :, pl.ds(part * 128 + begin, 64), :],
                        out_sem.at[n, a],
                    )
                )
                going[-1].start()
    for copy in going:
        copy.wait()


def unpack(slabs):
    return pl.pallas_call(
        unpack_kernel,
        in_specs=in_vmem(1) + in_hbm(1),
        out_specs=in_hbm(4),
        out_shape=[jax.ShapeDtypeStruct((1, 2, 256, D), BF16)] * 4,
        scratch_shapes=[
            pltpu.VMEM((8, 16, 16, D), BF16),
            pltpu.VMEM((2, 4, 2, 128, D), BF16),
            pltpu.SemaphoreType.DMA((8,)),
            pltpu.SemaphoreType.DMA((8, 4)),
        ],
        compiler_params=params(60),
        cost_estimate=pl.CostEstimate(
            flops=2 * 2048 * 256 * D, bytes_accessed=8192 * D, transcendentals=0
        ),
        name="unpack",
    )(const(order_to_slabs(2).T.copy()), slabs)


def halves_kernel(mine_hbm, other_hbm, own_hbm, s1, s2, s3, mine_ref, other_ref, send_ref, in_sem, out_sem):
    y = lax.axis_index("y")
    outs = (own_hbm, s1, s2, s3)
    coming, going = [], []
    for k in (1, 2, 3, 0):
        rows = pl.ds(pl.multiple_of((y ^ k) * 288, 32), 288)
        coming.append((
            pltpu.make_async_copy(mine_hbm.at[rows, :], mine_ref.at[k], in_sem.at[k, 0]),
            pltpu.make_async_copy(other_hbm.at[rows, :], other_ref.at[k], in_sem.at[k, 1]),
        ))
        for copy in coming[-1]:
            copy.start()
    for i, k in enumerate((1, 2, 3, 0)):
        for copy in coming[i]:
            copy.wait()
        total = mine_ref[k] + other_ref[k].astype(F32)
        if k == 0:
            mine_ref[k] = total
            source = mine_ref.at[k]
        else:
            send_ref[k - 1] = total.astype(BF16)
            source = send_ref.at[k - 1]
        going.append(pltpu.make_async_copy(source, outs[k], out_sem.at[k]))
        going[-1].start()
    for copy in going:
        copy.wait()


def halves(mine, other):
    return pl.pallas_call(
        halves_kernel,
        in_specs=in_hbm(2),
        out_specs=in_hbm(4),
        out_shape=[jax.ShapeDtypeStruct((288, 576), F32)] + [jax.ShapeDtypeStruct((288, 576), BF16)] * 3,
        scratch_shapes=[
            pltpu.VMEM((4, 288, 576), F32),
            pltpu.VMEM((4, 288, 576), BF16),
            pltpu.VMEM((3, 288, 576), BF16),
            pltpu.SemaphoreType.DMA((4, 2)),
            pltpu.SemaphoreType.DMA((4,)),
        ],
        compiler_params=params(60),
        cost_estimate=pl.CostEstimate(flops=D * 576, bytes_accessed=10 * D * 576, transcendentals=0),
        name="halves",
    )(mine, other)


SIZES = {"y": 4, "x": 4, "zl": 4, "zh": 2, "c": 2, ("zl", "zh"): 8}


def swap(value, axis, k):
    return lax.ppermute(value, axis, [(i, i ^ k) for i in range(SIZES[axis])])


def sum_over(blocks, axis):
    at = lax.axis_index(axis)
    total = lax.dynamic_index_in_dim(blocks, at, 0, keepdims=False)
    for k in range(1, SIZES[axis]):
        total = total + swap(lax.dynamic_index_in_dim(blocks, at ^ k, 0, keepdims=False), axis, k)
    return total


def weight_total(mine, theirs):
    own, *sent = halves(mine, swap(theirs, "c", 1))
    total = own
    for k in range(1, 4):
        total = total + swap(sent[k - 1], "y", k).astype(F32)
    blocks = total.reshape(4, 4, 18, 576).transpose(1, 0, 2, 3)
    blocks = sum_over(blocks, "x")
    blocks = blocks.reshape(4, 18, 2, 288).transpose(0, 2, 1, 3).reshape(8, 18, 288)
    return sum_over(blocks, ("zl", "zh")).T


def by_rank(axis, own, other):
    first = lax.axis_index(axis) == 0
    return jnp.stack([jnp.where(first, own, other), jnp.where(first, other, own)])


def whole_weight(out_weight):
    place = lax.axis_index("y") * 4 + lax.axis_index("x")
    piece = lax.dynamic_slice_in_dim(out_weight, place * 18, 18, 0)
    rows = lax.all_gather(piece, ("zh", "y", "x"), axis=0, tiled=False).reshape(2, 288, D)
    both = by_rank("c", rows, swap(rows, "c", 1))
    return both.transpose(1, 0, 2, 3).reshape(D, D)


def exchange(t):
    return lax.all_to_all(t, SEQ, split_axis=0, concat_axis=0, tiled=True)


def on_device(queries, keys, values, cotangent, out_weight):
    arrays = (queries, keys, values, cotangent)
    weight = whole_weight(out_weight)
    received = exchange(pack(arrays))
    by_patch, att, stats, mine, theirs = forward(received)
    weight_grad = weight_total(mine, theirs)
    sent = backward(by_patch, att, stats, weight)
    return (*unpack(exchange(sent)), weight_grad)


def solution(mesh):
    fine = Mesh(mesh.devices.reshape(4, 4, 4, 2, 2), ("y", "zl", "x", "zh", "c"))
    frames = P(ROWS, SEQ, None, None)
    return jax.shard_map(
        on_device,
        mesh=fine,
        in_specs=(frames, frames, frames, frames, P(ROWS, None)),
        out_specs=(frames, frames, frames, frames, P(ROWS, SEQ)),
        check_vma=False,
    )
```

```python
import functools

import jax
import jax.numpy as jnp
import numpy as np
from jax import lax
from jax.experimental import pallas as pl
from jax.experimental.pallas import tpu as pltpu
from jax.sharding import Mesh
from jax.sharding import PartitionSpec as P

HEADS = 16
HEAD_DIM = 72
D = 1152
SCALE = HEAD_DIM ** (-0.5)
LOG2E = 1.4426950408889634
MIB = 1024 * 1024
F32 = jnp.float32
BF16 = jnp.bfloat16
SEQ = ("y", "zl", "x")
ROWS = ("zh", "c")


def order_to_slabs(np_):
    size = 128 * np_
    out = np.zeros((size, size), np.float32)
    for s in range(16):
        for a in range(4):
            for f in range(2):
                for p in range(np_):
                    out[((s * 4 + a) * 2 + f) * np_ + p, ((a * 2 + f) * 16 + s) * np_ + p] = 1
    return out


def order_to_patches(np_):
    size = 128 * np_
    out = np.zeros((size, size), np.float32)
    for s in range(16):
        for a in range(4):
            for f in range(2):
                for p in range(np_):
                    out[((a * np_ + p) * 16 + s) * 2 + f, ((s * 4 + a) * 2 + f) * np_ + p] = 1
    return out


def const(matrix):
    return jnp.asarray(matrix, BF16)


def move(order, rows):
    return jnp.dot(order, rows, preferred_element_type=F32).astype(BF16)


def whole(shape):
    return pl.BlockSpec(shape, lambda i: (0,) * len(shape))


def params(mib):
    return pltpu.CompilerParams(vmem_limit_bytes=mib * MIB)


def in_hbm(count):
    return [pl.BlockSpec(memory_space=pltpu.HBM)] * count


def in_vmem(count):
    return [pl.BlockSpec(memory_space=pltpu.VMEM)] * count


def pack_kernel(order_ref, q_ref, k_ref, v_ref, c_ref, token, out_ref, rows_ref, slabs_ref, in_sem, out_sem):
    arrays = (q_ref, k_ref, v_ref, c_ref)
    coming, going = [], []
    for part in range(2):
        for a in range(4):
            coming.append(
                pltpu.make_async_copy(
                    arrays[a].at[0, :, pl.ds(part * 128, 128), :],
                    rows_ref.at[part, a],
                    in_sem.at[part, a],
                )
            )
            coming[-1].start()
    for part in range(2):
        for a in range(4):
            coming[4 * part + a].wait()
        for g in range(4):
            rows = [rows_ref[part, a, f, pl.ds(g * 32, 32), :] for a in range(4) for f in range(2)]
            slabs_ref[part, g] = move(order_ref[...], jnp.concatenate(rows, axis=0)).reshape(16, 16, D)
            going.append(
                pltpu.make_async_copy(
                    slabs_ref.at[part, g],
                    out_ref.at[pl.ds(g * 16, 16), pl.ds(part * 16, 16), :],
                    out_sem.at[part, g],
                )
            )
            going[-1].start()
    for copy in going:
        copy.wait()


def pack(arrays, token):
    return pl.pallas_call(
        pack_kernel,
        in_specs=in_vmem(1) + in_hbm(4) + [pl.BlockSpec(memory_space=pl.ANY)],
        out_specs=pl.BlockSpec(memory_space=pltpu.HBM),
        out_shape=jax.ShapeDtypeStruct((64, 32, D), BF16),
        scratch_shapes=[
            pltpu.VMEM((2, 4, 2, 128, D), BF16),
            pltpu.VMEM((2, 4, 16, 16, D), BF16),
            pltpu.SemaphoreType.DMA((2, 4)),
            pltpu.SemaphoreType.DMA((2, 4)),
        ],
        compiler_params=params(60),
        cost_estimate=pl.CostEstimate(
            flops=2 * 2048 * 256 * D, bytes_accessed=8192 * D, transcendentals=0
        ),
        name="pack",
    )(const(order_to_slabs(2)), *arrays, token)


def attend_part(part, order_ref, back_ref, r_ref, w_ref, s_ref, att_ref, cot_ref, *refs):
    in_ref, x_ref, u_ref, y_ref, out_ref, kept_ref, in_sem, out_sem, kept_sem = refs
    slots = pl.ds(pl.multiple_of(part * 16, 16), 16)
    mine = pl.ds(pl.multiple_of(part * 256, 256), 256)
    for b in range(4):
        n = part * 4 + b
        pltpu.make_async_copy(r_ref.at[pl.ds(b * 16, 16), slots, :], in_ref.at[n], in_sem.at[n]).wait()
        t = move(order_ref[...], in_ref[n].reshape(256, D))
        for a in range(4):
            for p in range(2):
                x_ref[a, pl.ds(p * 128 + b * 32, 32), :] = t[(a * 2 + p) * 32 : (a * 2 + p + 1) * 32]
    cot = x_ref[3]
    kept_ref[part, 1] = cot
    pltpu.make_async_copy(kept_ref.at[part, 1], cot_ref.at[mine, :], kept_sem.at[part, 1]).start()
    u_ref[...] = lax.dot_general(
        cot, w_ref[...], (((1,), (1,)), ((), ())), preferred_element_type=F32
    ).astype(BF16)
    y_ref[...] = jnp.zeros_like(y_ref)
    lane = lax.broadcasted_iota(jnp.int32, (1, 256), 1)
    for j in range(8):
        first = (lane >= 16 * j) & (lane < 16 * j + 72)
        second = (lane >= 16 * j + 72) & (lane < 16 * j + 144)
        keep_first = first.astype(F32).astype(BF16)
        keep_second = second.astype(F32).astype(BF16)
        win = pl.ds(128 * j, 256)

        def both(t):
            return jnp.concatenate([t * keep_first, t * keep_second], axis=0)

        def beside(t):
            return jnp.concatenate([t[:128], t[128:]], axis=1)

        for p in range(2):
            rows = pl.ds(p * 128, 128)
            q = x_ref[0, rows, win]
            u = u_ref[rows, win]
            kk = both(x_ref[1, rows, win])
            vv = both(x_ref[2, rows, win])
            scores = lax.dot_general(kk, q, (((1,), (1,)), ((), ())), preferred_element_type=F32)
            scores = scores.reshape(2, 128, 128)
            top = jnp.max(scores, axis=1, keepdims=True)
            raised = jnp.exp2((scores - top) * (SCALE * LOG2E))
            prob = raised * (1.0 / jnp.sum(raised, axis=1, keepdims=True))
            low = prob.astype(BF16).reshape(256, 128)
            grad = lax.dot_general(vv, u, (((1,), (1,)), ((), ())), preferred_element_type=F32)
            grad = grad.reshape(2, 128, 128)
            centre = jnp.sum(prob * grad, axis=1, keepdims=True)
            sg = (prob * (grad - centre) * SCALE).astype(BF16).reshape(256, 128)
            y_ref[0, rows, win] += lax.dot_general(
                low, vv, (((0,), (0,)), ((), ())), preferred_element_type=F32
            ).astype(BF16)
            y_ref[1, rows, win] += lax.dot_general(
                sg, kk, (((0,), (0,)), ((), ())), preferred_element_type=F32
            ).astype(BF16)
            y_ref[2, rows, win] += jnp.dot(
                beside(sg), both(q), preferred_element_type=F32
            ).astype(BF16)
            y_ref[3, rows, win] += jnp.dot(
                beside(low), both(u), preferred_element_type=F32
            ).astype(BF16)
    att = y_ref[0]
    kept_ref[part, 0] = att
    pltpu.make_async_copy(kept_ref.at[part, 0], att_ref.at[mine, :], kept_sem.at[part, 0]).start()
    y_ref[0] = jnp.dot(att, w_ref[...], preferred_element_type=F32).astype(BF16)
    for b in range(4):
        n = part * 4 + b
        t = jnp.concatenate(
            [y_ref[a, pl.ds(p * 128 + b * 32, 32), :] for a in range(4) for p in range(2)], axis=0
        )
        out_ref[n] = move(back_ref[...], t).reshape(16, 16, D)
        pltpu.make_async_copy(out_ref.at[n], s_ref.at[pl.ds(b * 16, 16), slots, :], out_sem.at[n]).start()


def attend_kernel(*refs):
    r_ref, s_ref, att_ref, cot_ref = refs[2], refs[4], refs[5], refs[6]
    in_ref, out_ref, kept_ref, in_sem, out_sem, kept_sem = refs[7], *refs[11:]
    for n in range(8):
        part, b = divmod(n, 4)
        pltpu.make_async_copy(
            r_ref.at[pl.ds(b * 16, 16), pl.ds(part * 16, 16), :], in_ref.at[n], in_sem.at[n]
        ).start()

    @pl.loop(0, 2)
    def _(part):
        attend_part(part, *refs)

    for part in range(2):
        for i, ref in enumerate((att_ref, cot_ref)):
            pltpu.make_async_copy(
                kept_ref.at[part, i], ref.at[pl.ds(part * 256, 256), :], kept_sem.at[part, i]
            ).wait()
        for b in range(4):
            n = part * 4 + b
            pltpu.make_async_copy(
                out_ref.at[n], s_ref.at[pl.ds(b * 16, 16), pl.ds(part * 16, 16), :], out_sem.at[n]
            ).wait()


def attend(received, weight):
    order = order_to_patches(2)
    return pl.pallas_call(
        attend_kernel,
        in_specs=in_vmem(2) + in_hbm(1) + in_vmem(1),
        out_specs=in_hbm(3),
        out_shape=[
            jax.ShapeDtypeStruct((64, 32, D), BF16),
            jax.ShapeDtypeStruct((512, D), BF16),
            jax.ShapeDtypeStruct((512, D), BF16),
        ],
        scratch_shapes=[
            pltpu.VMEM((8, 16, 16, D), BF16),
            pltpu.VMEM((4, 256, D), BF16),
            pltpu.VMEM((256, D), BF16),
            pltpu.VMEM((4, 256, D), BF16),
            pltpu.VMEM((8, 16, 16, D), BF16),
            pltpu.VMEM((2, 2, 256, D), BF16),
            pltpu.SemaphoreType.DMA((8,)),
            pltpu.SemaphoreType.DMA((8,)),
            pltpu.SemaphoreType.DMA((2, 2)),
        ],
        compiler_params=params(58),
        cost_estimate=pl.CostEstimate(
            flops=12_000_000_000, bytes_accessed=40 * 256 * D + 2 * D * D, transcendentals=1048576
        ),
        name="attend",
    )(const(order), const(order.T.copy()), received, weight)


def unpack_kernel(order_ref, slabs_ref, *refs):
    outs = refs[:4]
    in_ref, rows_ref, in_sem, out_sem = refs[4:]
    coming, going = [], []
    for n in range(8):
        part, g = divmod(n, 4)
        coming.append(
            pltpu.make_async_copy(
                slabs_ref.at[pl.ds(g * 16, 16), pl.ds(part * 16, 16), :], in_ref.at[n], in_sem.at[n]
            )
        )
        coming[-1].start()
    for n in range(8):
        part, g = divmod(n, 4)
        coming[n].wait()
        t = move(order_ref[...], in_ref[n].reshape(256, D))
        for a in range(4):
            for f in range(2):
                at = (a * 2 + f) * 32
                rows_ref[part, a, f, pl.ds(g * 32, 32), :] = t[at : at + 32]
            if g % 2 == 1:
                begin = (g - 1) * 32
                going.append(
                    pltpu.make_async_copy(
                        rows_ref.at[part, a, :, pl.ds(begin, 64), :],
                        outs[a].at[0, :, pl.ds(part * 128 + begin, 64), :],
                        out_sem.at[n, a],
                    )
                )
                going[-1].start()
    for copy in going:
        copy.wait()


def unpack(slabs):
    return pl.pallas_call(
        unpack_kernel,
        in_specs=in_vmem(1) + in_hbm(1),
        out_specs=in_hbm(4),
        out_shape=[jax.ShapeDtypeStruct((1, 2, 256, D), BF16)] * 4,
        scratch_shapes=[
            pltpu.VMEM((8, 16, 16, D), BF16),
            pltpu.VMEM((2, 4, 2, 128, D), BF16),
            pltpu.SemaphoreType.DMA((8,)),
            pltpu.SemaphoreType.DMA((8, 4)),
        ],
        compiler_params=params(60),
        cost_estimate=pl.CostEstimate(
            flops=2 * 2048 * 256 * D, bytes_accessed=8192 * D, transcendentals=0
        ),
        name="unpack",
    )(const(order_to_slabs(2).T.copy()), slabs)


def outer_kernel(turn_ref, att_ref, cot_ref, mine_ref, theirs_ref):
    att = att_ref[...]
    cot = cot_ref[...]
    turned = move(cot, turn_ref[...])
    parts = [att[:, 288 * b : 288 * b + 288] for b in range(4)]
    core = lax.axis_index("c")

    def product(left, even, odd):
        chosen = jnp.where(core == 0, even, odd)
        return lax.dot_general(left, chosen, (((0,), (0,)), ((), ())), preferred_element_type=F32)

    theirs_ref[:, :288] = product(cot, parts[1], parts[0]).astype(BF16)
    theirs_ref[:, 288:] = product(turned, parts[3], parts[2]).astype(BF16)
    mine_ref[:, :288] = product(cot, parts[0], parts[1])
    mine_ref[:, 288:] = product(turned, parts[2], parts[3])


def turn():
    order = np.arange(D).reshape(4, 4, 4, 18).transpose(2, 0, 1, 3).reshape(-1)
    out = np.zeros((D, D), np.float32)
    out[order, np.arange(D)] = 1
    return const(out)


def outer(att, cot):
    return pl.pallas_call(
        outer_kernel,
        in_specs=in_vmem(3),
        out_specs=in_vmem(2),
        out_shape=[jax.ShapeDtypeStruct((D, 576), F32), jax.ShapeDtypeStruct((D, 576), BF16)],
        compiler_params=params(24),
        cost_estimate=pl.CostEstimate(
            flops=2 * 512 * D * D, bytes_accessed=4 * 512 * D + 6 * D * 576, transcendentals=0
        ),
        name="outer",
    )(turn(), att, cot)


def halves_kernel(mine_ref, other_ref, own_ref, *out_refs):
    for i, axis in enumerate(("y", "x")):
        columns = slice(288 * i, 288 * i + 288)
        at = lax.axis_index(axis)
        for k in range(4):
            rows = pl.ds(pl.multiple_of((at ^ k) * 288, 32), 288)
            total = mine_ref[rows, columns] + other_ref[rows, columns].astype(F32)
            if k == 0:
                own_ref[i] = total
            else:
                out_refs[3 * i + k - 1][...] = total.astype(BF16)


def halves(mine, other):
    return pl.pallas_call(
        halves_kernel,
        in_specs=in_vmem(2),
        out_specs=in_vmem(7),
        out_shape=[jax.ShapeDtypeStruct((2, 288, 288), F32)] + [jax.ShapeDtypeStruct((288, 288), BF16)] * 6,
        compiler_params=params(24),
        cost_estimate=pl.CostEstimate(flops=D * 576, bytes_accessed=10 * D * 576, transcendentals=0),
        name="halves",
    )(mine, other)


SIZES = {"y": 4, "x": 4, "zl": 4, "zh": 2, "c": 2, ("zl", "zh"): 8}


def swap(value, axis, k):
    return lax.ppermute(value, axis, [(i, i ^ k) for i in range(SIZES[axis])])


def terms_over(blocks, axis):
    at = lax.axis_index(axis)
    own = lax.dynamic_index_in_dim(blocks, at, 0, keepdims=False)
    return [own] + [
        swap(lax.dynamic_index_in_dim(blocks, at ^ k, 0, keepdims=False), axis, k)
        for k in range(1, SIZES[axis])
    ]


def weight_terms(att, cot):
    mine, theirs = outer(att, cot)
    own, *sent = halves(mine, swap(theirs, "c", 1))
    here, there = own[0], own[1]
    for k in range(1, 4):
        here = here + swap(sent[k - 1], "y", k).astype(F32)
        there = there + swap(sent[k + 2], "x", k).astype(F32)
    here = sum(terms_over(here.reshape(4, 4, 18, 288).transpose(1, 0, 2, 3), "x"))
    there = sum(terms_over(there.reshape(4, 4, 18, 288), "y"))
    return terms_over(jnp.stack([here, there], axis=1).reshape(8, 18, 288), ("zl", "zh"))


def add_up_kernel(*refs):
    total = refs[0][...]
    for ref in refs[1:8]:
        total = total + ref[...]
    refs[-1][...] = total


def add_up(terms, token):
    return pl.pallas_call(
        add_up_kernel,
        in_specs=in_vmem(8) + [pl.BlockSpec(memory_space=pl.ANY)],
        out_specs=pl.BlockSpec(memory_space=pltpu.VMEM),
        out_shape=jax.ShapeDtypeStruct((18, 288), F32),
        compiler_params=params(8),
        name="add_up",
    )(*terms, token)


def by_rank(axis, own, other):
    first = lax.axis_index(axis) == 0
    return jnp.stack([jnp.where(first, own, other), jnp.where(first, other, own)])


def whole_weight(piece, other):
    pair = by_rank("zh", piece, other)
    rows = lax.all_gather(pair, ("y", "x"), axis=0, tiled=False)
    rows = rows.transpose(1, 0, 2, 3).reshape(2, 288, D)
    both = by_rank("c", rows, swap(rows, "c", 1))
    return both.transpose(1, 0, 2, 3).reshape(D, D)


def exchange(t):
    return lax.all_to_all(t, SEQ, split_axis=0, concat_axis=0, tiled=True)


def on_device(queries, keys, values, cotangent, out_weight):
    arrays = (queries, keys, values, cotangent)
    place = lax.axis_index("y") * 4 + lax.axis_index("x")
    piece = lax.dynamic_slice_in_dim(out_weight, place * 18, 18, 0)
    other = swap(piece, "zh", 1)
    received = exchange(pack(arrays, other))
    sent, att, cot = attend(received, whole_weight(piece, other))
    terms = weight_terms(att, cot)
    outs = unpack(exchange(sent))
    return (*outs, add_up(terms, outs[0]).T)


def solution(mesh):
    fine = Mesh(mesh.devices.reshape(4, 4, 4, 2, 2), ("y", "zl", "x", "zh", "c"))
    frames = P(ROWS, SEQ, None, None)
    return jax.shard_map(
        on_device,
        mesh=fine,
        in_specs=(frames, frames, frames, frames, P(ROWS, None)),
        out_specs=(frames, frames, frames, frames, P(ROWS, SEQ)),
        check_vma=False,
    )
```

```python
import functools

import jax
import jax.numpy as jnp
import numpy as np
from jax import lax
from jax.experimental import pallas as pl
from jax.experimental.pallas import tpu as pltpu
from jax.sharding import Mesh
from jax.sharding import PartitionSpec as P

HEADS = 16
HEAD_DIM = 72
D = 1152
SCALE = HEAD_DIM ** (-0.5)
LOG2E = 1.4426950408889634
MIB = 1024 * 1024
F32 = jnp.float32
BF16 = jnp.bfloat16
SEQ = ("y", "zl", "x")
ROWS = ("zh", "c")


def order_to_slabs(np_):
    size = 128 * np_
    out = np.zeros((size, size), np.float32)
    for s in range(16):
        for a in range(4):
            for f in range(2):
                for p in range(np_):
                    out[((s * 4 + a) * 2 + f) * np_ + p, ((a * 2 + f) * 16 + s) * np_ + p] = 1
    return out


def order_to_patches(np_):
    size = 128 * np_
    out = np.zeros((size, size), np.float32)
    for s in range(16):
        for a in range(4):
            for f in range(2):
                for p in range(np_):
                    out[((a * np_ + p) * 16 + s) * 2 + f, ((s * 4 + a) * 2 + f) * np_ + p] = 1
    return out


def const(matrix):
    return jnp.asarray(matrix, BF16)


def move(order, rows):
    return jnp.dot(order, rows, preferred_element_type=F32).astype(BF16)


def whole(shape):
    return pl.BlockSpec(shape, lambda i: (0,) * len(shape))


def params(mib):
    return pltpu.CompilerParams(vmem_limit_bytes=mib * MIB)


def in_hbm(count):
    return [pl.BlockSpec(memory_space=pltpu.HBM)] * count


def in_vmem(count):
    return [pl.BlockSpec(memory_space=pltpu.VMEM)] * count


def pack_kernel(part, order_ref, q_ref, k_ref, v_ref, c_ref, *refs):
    out_ref, rows_ref, slabs_ref, in_sem, out_sem = refs[-5:]
    arrays = (q_ref, k_ref, v_ref, c_ref)
    coming, going = [], []
    for a in range(4):
        coming.append(
            pltpu.make_async_copy(
                arrays[a].at[0, :, pl.ds(part * 128, 128), :], rows_ref.at[a], in_sem.at[a]
            )
        )
        coming[-1].start()
    for copy in coming:
        copy.wait()
    for g in range(4):
        rows = [rows_ref[a, f, pl.ds(g * 32, 32), :] for a in range(4) for f in range(2)]
        slabs_ref[g] = move(order_ref[...], jnp.concatenate(rows, axis=0)).reshape(16, 16, D)
        going.append(
            pltpu.make_async_copy(slabs_ref.at[g], out_ref.at[pl.ds(g * 16, 16)], out_sem.at[g])
        )
        going[-1].start()
    for copy in going:
        copy.wait()


def pack(part, arrays, tokens):
    return pl.pallas_call(
        functools.partial(pack_kernel, part),
        in_specs=in_vmem(1) + in_hbm(4) + [pl.BlockSpec(memory_space=pl.ANY)] * len(tokens),
        out_specs=pl.BlockSpec(memory_space=pltpu.HBM),
        out_shape=jax.ShapeDtypeStruct((64, 16, D), BF16),
        scratch_shapes=[
            pltpu.VMEM((4, 2, 128, D), BF16),
            pltpu.VMEM((4, 16, 16, D), BF16),
            pltpu.SemaphoreType.DMA((4,)),
            pltpu.SemaphoreType.DMA((4,)),
        ],
        compiler_params=params(60),
        cost_estimate=pl.CostEstimate(
            flops=2 * 1024 * 256 * D, bytes_accessed=4096 * D, transcendentals=0
        ),
        name="pack",
    )(const(order_to_slabs(2)), *arrays, *tokens)


def attend_kernel(
    order_ref, back_ref, r_ref, w_ref, s_ref, att_ref, cot_ref,
    in_ref, x_ref, u_ref, y_ref, out_ref, kept_ref, in_sem, out_sem, kept_sem,
):
    coming = [
        pltpu.make_async_copy(r_ref.at[pl.ds(b * 16, 16)], in_ref.at[b], in_sem.at[b]) for b in range(4)
    ]
    for copy in coming:
        copy.start()
    for b in range(4):
        coming[b].wait()
        t = move(order_ref[...], in_ref[b].reshape(256, D))
        for a in range(4):
            for p in range(2):
                x_ref[a, pl.ds(p * 128 + b * 32, 32), :] = t[(a * 2 + p) * 32 : (a * 2 + p + 1) * 32]
    cot = x_ref[3]
    going = [pltpu.make_async_copy(x_ref.at[3], cot_ref, kept_sem.at[0])]
    going[-1].start()
    u_ref[...] = lax.dot_general(
        cot, w_ref[...], (((1,), (1,)), ((), ())), preferred_element_type=F32
    ).astype(BF16)
    y_ref[...] = jnp.zeros_like(y_ref)
    lane = lax.broadcasted_iota(jnp.int32, (1, 256), 1)
    for j in range(8):
        first = (lane >= 16 * j) & (lane < 16 * j + 72)
        second = (lane >= 16 * j + 72) & (lane < 16 * j + 144)
        keep_first = first.astype(F32).astype(BF16)
        keep_second = second.astype(F32).astype(BF16)
        win = pl.ds(128 * j, 256)

        def both(t):
            return jnp.concatenate([t * keep_first, t * keep_second], axis=0)

        def beside(t):
            return jnp.concatenate([t[:128], t[128:]], axis=1)

        for p in range(2):
            rows = pl.ds(p * 128, 128)
            q = x_ref[0, rows, win]
            u = u_ref[rows, win]
            kk = both(x_ref[1, rows, win])
            vv = both(x_ref[2, rows, win])
            scores = lax.dot_general(kk, q, (((1,), (1,)), ((), ())), preferred_element_type=F32)
            scores = scores.reshape(2, 128, 128)
            top = jnp.max(scores, axis=1, keepdims=True)
            raised = jnp.exp2((scores - top) * (SCALE * LOG2E))
            prob = raised * (1.0 / jnp.sum(raised, axis=1, keepdims=True))
            low = prob.astype(BF16).reshape(256, 128)
            grad = lax.dot_general(vv, u, (((1,), (1,)), ((), ())), preferred_element_type=F32)
            grad = grad.reshape(2, 128, 128)
            centre = jnp.sum(prob * grad, axis=1, keepdims=True)
            sg = (prob * (grad - centre) * SCALE).astype(BF16).reshape(256, 128)
            y_ref[0, rows, win] += lax.dot_general(
                low, vv, (((0,), (0,)), ((), ())), preferred_element_type=F32
            ).astype(BF16)
            y_ref[1, rows, win] += lax.dot_general(
                sg, kk, (((0,), (0,)), ((), ())), preferred_element_type=F32
            ).astype(BF16)
            y_ref[2, rows, win] += jnp.dot(
                beside(sg), both(q), preferred_element_type=F32
            ).astype(BF16)
            y_ref[3, rows, win] += jnp.dot(
                beside(low), both(u), preferred_element_type=F32
            ).astype(BF16)
    att = y_ref[0]
    kept_ref[...] = att
    going.append(pltpu.make_async_copy(kept_ref, att_ref, kept_sem.at[1]))
    going[-1].start()
    y_ref[0] = jnp.dot(att, w_ref[...], preferred_element_type=F32).astype(BF16)
    for b in range(4):
        t = jnp.concatenate(
            [y_ref[a, pl.ds(p * 128 + b * 32, 32), :] for a in range(4) for p in range(2)], axis=0
        )
        out_ref[b] = move(back_ref[...], t).reshape(16, 16, D)
        going.append(pltpu.make_async_copy(out_ref.at[b], s_ref.at[pl.ds(b * 16, 16)], out_sem.at[b]))
        going[-1].start()
    for copy in going:
        copy.wait()


def attend(received, weight):
    order = order_to_patches(2)
    return pl.pallas_call(
        attend_kernel,
        in_specs=in_vmem(2) + in_hbm(1) + in_vmem(1),
        out_specs=in_hbm(3),
        out_shape=[
            jax.ShapeDtypeStruct((64, 16, D), BF16),
            jax.ShapeDtypeStruct((256, D), BF16),
            jax.ShapeDtypeStruct((256, D), BF16),
        ],
        scratch_shapes=[
            pltpu.VMEM((4, 16, 16, D), BF16),
            pltpu.VMEM((4, 256, D), BF16),
            pltpu.VMEM((256, D), BF16),
            pltpu.VMEM((4, 256, D), BF16),
            pltpu.VMEM((4, 16, 16, D), BF16),
            pltpu.VMEM((256, D), BF16),
            pltpu.SemaphoreType.DMA((4,)),
            pltpu.SemaphoreType.DMA((4,)),
            pltpu.SemaphoreType.DMA((2,)),
        ],
        compiler_params=params(58),
        cost_estimate=pl.CostEstimate(
            flops=6_000_000_000, bytes_accessed=20 * 256 * D + 2 * D * D, transcendentals=524288
        ),
        name="attend",
    )(const(order), const(order.T.copy()), received, weight)


def unpack_kernel(part, order_ref, slabs_ref, *refs):
    outs = refs[-8:-4]
    in_ref, rows_ref, in_sem, out_sem = refs[-4:]
    coming, going = [], []
    for g in range(4):
        coming.append(
            pltpu.make_async_copy(slabs_ref.at[pl.ds(g * 16, 16)], in_ref.at[g], in_sem.at[g])
        )
        coming[-1].start()
    for g in range(4):
        coming[g].wait()
        t = move(order_ref[...], in_ref[g].reshape(256, D))
        for a in range(4):
            for f in range(2):
                at = (a * 2 + f) * 32
                rows_ref[g, a, f] = t[at : at + 32]
            going.append(
                pltpu.make_async_copy(
                    rows_ref.at[g, a],
                    outs[a].at[0, :, pl.ds(part * 128 + g * 32, 32), :],
                    out_sem.at[g, a],
                )
            )
            going[-1].start()
    for copy in going:
        copy.wait()


def unpack(part, slabs, before):
    return pl.pallas_call(
        functools.partial(unpack_kernel, part),
        in_specs=in_vmem(1) + in_hbm(1 + len(before)),
        out_specs=in_hbm(4),
        out_shape=[jax.ShapeDtypeStruct((1, 2, 256, D), BF16)] * 4,
        scratch_shapes=[
            pltpu.VMEM((4, 16, 16, D), BF16),
            pltpu.VMEM((4, 4, 2, 32, D), BF16),
            pltpu.SemaphoreType.DMA((4,)),
            pltpu.SemaphoreType.DMA((4, 4)),
        ],
        input_output_aliases={2 + a: a for a in range(len(before))},
        compiler_params=params(60),
        cost_estimate=pl.CostEstimate(
            flops=2 * 1024 * 256 * D, bytes_accessed=4096 * D, transcendentals=0
        ),
        name="unpack",
    )(const(order_to_slabs(2).T.copy()), slabs, *before)


def outer_kernel(turn_ref, att0_ref, att1_ref, cot0_ref, cot1_ref, mine_ref, theirs_ref):
    att = jnp.concatenate([att0_ref[...], att1_ref[...]], axis=0)
    cot = jnp.concatenate([cot0_ref[...], cot1_ref[...]], axis=0)
    turned = move(cot, turn_ref[...])
    parts = [att[:, 288 * b : 288 * b + 288] for b in range(4)]
    core = lax.axis_index("c")

    def product(left, even, odd):
        chosen = jnp.where(core == 0, even, odd)
        return lax.dot_general(left, chosen, (((0,), (0,)), ((), ())), preferred_element_type=F32)

    theirs_ref[:, :288] = product(cot, parts[1], parts[0]).astype(BF16)
    theirs_ref[:, 288:] = product(turned, parts[3], parts[2]).astype(BF16)
    mine_ref[:, :288] = product(cot, parts[0], parts[1])
    mine_ref[:, 288:] = product(turned, parts[2], parts[3])


def turn():
    order = np.arange(D).reshape(4, 4, 4, 18).transpose(2, 0, 1, 3).reshape(-1)
    out = np.zeros((D, D), np.float32)
    out[order, np.arange(D)] = 1
    return const(out)


def outer(atts, cots):
    return pl.pallas_call(
        outer_kernel,
        in_specs=in_vmem(5),
        out_specs=in_vmem(2),
        out_shape=[jax.ShapeDtypeStruct((D, 576), F32), jax.ShapeDtypeStruct((D, 576), BF16)],
        compiler_params=params(24),
        cost_estimate=pl.CostEstimate(
            flops=2 * 512 * D * D, bytes_accessed=4 * 512 * D + 6 * D * 576, transcendentals=0
        ),
        name="outer",
    )(turn(), *atts, *cots)


def halves_kernel(mine_ref, other_ref, own_ref, *out_refs):
    for i, axis in enumerate(("y", "x")):
        columns = slice(288 * i, 288 * i + 288)
        at = lax.axis_index(axis)
        for k in range(4):
            rows = pl.ds(pl.multiple_of((at ^ k) * 288, 32), 288)
            total = mine_ref[rows, columns] + other_ref[rows, columns].astype(F32)
            if k == 0:
                own_ref[i] = total
            else:
                out_refs[3 * i + k - 1][...] = total.astype(BF16)


def halves(mine, other):
    return pl.pallas_call(
        halves_kernel,
        in_specs=in_vmem(2),
        out_specs=in_vmem(7),
        out_shape=[jax.ShapeDtypeStruct((2, 288, 288), F32)] + [jax.ShapeDtypeStruct((288, 288), BF16)] * 6,
        compiler_params=params(24),
        cost_estimate=pl.CostEstimate(flops=D * 576, bytes_accessed=10 * D * 576, transcendentals=0),
        name="halves",
    )(mine, other)


SIZES = {"y": 4, "x": 4, "zl": 4, "zh": 2, "c": 2, ("zl", "zh"): 8}


def swap(value, axis, k):
    return lax.ppermute(value, axis, [(i, i ^ k) for i in range(SIZES[axis])])


def terms_over(blocks, axis):
    at = lax.axis_index(axis)
    own = lax.dynamic_index_in_dim(blocks, at, 0, keepdims=False)
    return [own] + [
        swap(lax.dynamic_index_in_dim(blocks, at ^ k, 0, keepdims=False), axis, k)
        for k in range(1, SIZES[axis])
    ]


def weight_terms(atts, cots):
    mine, theirs = outer(atts, cots)
    own, *sent = halves(mine, swap(theirs, "c", 1))
    here, there = own[0], own[1]
    for k in range(1, 4):
        here = here + swap(sent[k - 1], "y", k).astype(F32)
        there = there + swap(sent[k + 2], "x", k).astype(F32)
    first = [here, there]
    here = sum(terms_over(here.reshape(4, 4, 18, 288).transpose(1, 0, 2, 3), "x"))
    there = sum(terms_over(there.reshape(4, 4, 18, 288), "y"))
    return first, terms_over(jnp.stack([here, there], axis=1).reshape(8, 18, 288), ("zl", "zh"))


def add_up_kernel(*refs):
    total = refs[0][...]
    for ref in refs[1:8]:
        total = total + ref[...]
    refs[-1][...] = total


def add_up(terms, token):
    return pl.pallas_call(
        add_up_kernel,
        in_specs=in_vmem(8) + [pl.BlockSpec(memory_space=pl.ANY)],
        out_specs=pl.BlockSpec(memory_space=pltpu.VMEM),
        out_shape=jax.ShapeDtypeStruct((18, 288), F32),
        compiler_params=params(8),
        name="add_up",
    )(*terms, token)


def by_rank(axis, own, other):
    first = lax.axis_index(axis) == 0
    return jnp.stack([jnp.where(first, own, other), jnp.where(first, other, own)])


def whole_weight(piece, other):
    pair = by_rank("zh", piece, other)
    rows = lax.all_gather(pair, ("y", "x"), axis=0, tiled=False)
    rows = rows.transpose(1, 0, 2, 3).reshape(2, 288, D)
    both = by_rank("c", rows, swap(rows, "c", 1))
    return both.transpose(1, 0, 2, 3).reshape(D, D)


def hold_kernel(*refs):
    pass


def hold(value, tokens):
    return pl.pallas_call(
        hold_kernel,
        in_specs=[pl.BlockSpec(memory_space=pl.ANY)] * (1 + len(tokens)),
        out_specs=pl.BlockSpec(memory_space=pl.ANY),
        out_shape=jax.ShapeDtypeStruct(value.shape, value.dtype),
        input_output_aliases={0: 0},
        name="hold",
    )(value, *tokens)


def exchange(t):
    return lax.all_to_all(t, SEQ, split_axis=0, concat_axis=0, tiled=True)


def on_device(queries, keys, values, cotangent, out_weight):
    arrays = (queries, keys, values, cotangent)
    place = lax.axis_index("y") * 4 + lax.axis_index("x")
    piece = lax.dynamic_slice_in_dim(out_weight, place * 18, 18, 0)
    other = swap(piece, "zh", 1)
    received = [exchange(hold(pack(0, arrays, []), [other])), exchange(pack(1, arrays, []))]
    weight = whole_weight(piece, other)
    sent, atts, cots = zip(*[attend(t, weight) for t in received])
    begun, terms = weight_terms(atts, cots)
    outs = unpack(0, exchange(sent[0]), ())
    outs = unpack(1, exchange(hold(sent[1], begun)), outs)
    return (*outs, add_up(terms, outs[0]).T)


def solution(mesh):
    fine = Mesh(mesh.devices.reshape(4, 4, 4, 2, 2), ("y", "zl", "x", "zh", "c"))
    frames = P(ROWS, SEQ, None, None)
    return jax.shard_map(
        on_device,
        mesh=fine,
        in_specs=(frames, frames, frames, frames, P(ROWS, None)),
        out_specs=(frames, frames, frames, frames, P(ROWS, SEQ)),
        check_vma=False,
    )
```

```python
import functools

import jax
import jax.numpy as jnp
import numpy as np
from jax import lax
from jax.experimental import pallas as pl
from jax.experimental.pallas import tpu as pltpu
from jax.sharding import Mesh
from jax.sharding import PartitionSpec as P

HEADS = 16
HEAD_DIM = 72
D = 1152
SCALE = HEAD_DIM ** (-0.5)
LOG2E = 1.4426950408889634
MIB = 1024 * 1024
F32 = jnp.float32
BF16 = jnp.bfloat16
SEQ = ("y", "zl", "x")
ROWS = ("zh", "c")


def order_to_slabs(np_):
    size = 128 * np_
    out = np.zeros((size, size), np.float32)
    for s in range(16):
        for a in range(4):
            for f in range(2):
                for p in range(np_):
                    out[((s * 4 + a) * 2 + f) * np_ + p, ((a * 2 + f) * 16 + s) * np_ + p] = 1
    return out


def order_to_patches(np_):
    size = 128 * np_
    out = np.zeros((size, size), np.float32)
    for s in range(16):
        for a in range(4):
            for f in range(2):
                for p in range(np_):
                    out[((a * np_ + p) * 16 + s) * 2 + f, ((s * 4 + a) * 2 + f) * np_ + p] = 1
    return out


def const(matrix):
    return jnp.asarray(matrix, BF16)


def move(order, rows):
    return jnp.dot(order, rows, preferred_element_type=F32).astype(BF16)


def whole(shape):
    return pl.BlockSpec(shape, lambda i: (0,) * len(shape))


def params(mib):
    return pltpu.CompilerParams(vmem_limit_bytes=mib * MIB)


def in_hbm(count):
    return [pl.BlockSpec(memory_space=pltpu.HBM)] * count


def in_vmem(count):
    return [pl.BlockSpec(memory_space=pltpu.VMEM)] * count


def pack_kernel(part, order_ref, q_ref, k_ref, v_ref, c_ref, *refs):
    out_ref, rows_ref, slabs_ref, in_sem, out_sem = refs[-5:]
    arrays = (q_ref, k_ref, v_ref, c_ref)
    coming, going = [], []
    for a in range(4):
        coming.append(
            pltpu.make_async_copy(
                arrays[a].at[0, :, pl.ds(part * 128, 128), :], rows_ref.at[a], in_sem.at[a]
            )
        )
        coming[-1].start()
    for copy in coming:
        copy.wait()
    for g in range(4):
        rows = [rows_ref[a, f, pl.ds(g * 32, 32), :] for a in range(4) for f in range(2)]
        slabs_ref[g] = move(order_ref[...], jnp.concatenate(rows, axis=0)).reshape(16, 16, D)
        going.append(
            pltpu.make_async_copy(slabs_ref.at[g], out_ref.at[pl.ds(g * 16, 16)], out_sem.at[g])
        )
        going[-1].start()
    for copy in going:
        copy.wait()


def pack(part, arrays, tokens):
    return pl.pallas_call(
        functools.partial(pack_kernel, part),
        in_specs=in_vmem(1) + in_hbm(4) + [pl.BlockSpec(memory_space=pl.ANY)] * len(tokens),
        out_specs=pl.BlockSpec(memory_space=pltpu.HBM),
        out_shape=jax.ShapeDtypeStruct((64, 16, D), BF16),
        scratch_shapes=[
            pltpu.VMEM((4, 2, 128, D), BF16),
            pltpu.VMEM((4, 16, 16, D), BF16),
            pltpu.SemaphoreType.DMA((4,)),
            pltpu.SemaphoreType.DMA((4,)),
        ],
        compiler_params=params(60),
        cost_estimate=pl.CostEstimate(
            flops=2 * 1024 * 256 * D, bytes_accessed=4096 * D, transcendentals=0
        ),
        name="pack",
    )(const(order_to_slabs(2)), *arrays, *tokens)


def attend_kernel(
    order_ref, back_ref, r_ref, w_ref, s_ref, att_ref, cot_ref,
    in_ref, x_ref, u_ref, y_ref, out_ref, kept_ref, in_sem, out_sem, kept_sem,
):
    coming = [
        pltpu.make_async_copy(r_ref.at[pl.ds(b * 16, 16)], in_ref.at[b], in_sem.at[b]) for b in range(4)
    ]
    for copy in coming:
        copy.start()
    for b in range(4):
        coming[b].wait()
        t = move(order_ref[...], in_ref[b].reshape(256, D))
        for a in range(4):
            for p in range(2):
                x_ref[a, pl.ds(p * 128 + b * 32, 32), :] = t[(a * 2 + p) * 32 : (a * 2 + p + 1) * 32]
    cot = x_ref[3]
    going = [pltpu.make_async_copy(x_ref.at[3], cot_ref, kept_sem.at[0])]
    going[-1].start()
    u_ref[...] = lax.dot_general(
        cot, w_ref[...], (((1,), (1,)), ((), ())), preferred_element_type=F32
    ).astype(BF16)
    y_ref[...] = jnp.zeros_like(y_ref)
    lane = lax.broadcasted_iota(jnp.int32, (1, 256), 1)
    for j in range(8):
        first = (lane >= 16 * j) & (lane < 16 * j + 72)
        second = (lane >= 16 * j + 72) & (lane < 16 * j + 144)
        keep_first = first.astype(F32).astype(BF16)
        keep_second = second.astype(F32).astype(BF16)
        win = pl.ds(128 * j, 256)

        def both(t):
            return jnp.concatenate([t * keep_first, t * keep_second], axis=0)

        def beside(t):
            return jnp.concatenate([t[:128], t[128:]], axis=1)

        for p in range(2):
            rows = pl.ds(p * 128, 128)
            q = x_ref[0, rows, win]
            u = u_ref[rows, win]
            kk = both(x_ref[1, rows, win])
            vv = both(x_ref[2, rows, win])
            scores = lax.dot_general(kk, q, (((1,), (1,)), ((), ())), preferred_element_type=F32)
            scores = scores.reshape(2, 128, 128)
            top = jnp.max(scores, axis=1, keepdims=True)
            raised = jnp.exp2((scores - top) * (SCALE * LOG2E))
            prob = raised * (1.0 / jnp.sum(raised, axis=1, keepdims=True))
            low = prob.astype(BF16).reshape(256, 128)
            grad = lax.dot_general(vv, u, (((1,), (1,)), ((), ())), preferred_element_type=F32)
            grad = grad.reshape(2, 128, 128)
            centre = jnp.sum(prob * grad, axis=1, keepdims=True)
            sg = (prob * (grad - centre) * SCALE).astype(BF16).reshape(256, 128)
            y_ref[0, rows, win] += lax.dot_general(
                low, vv, (((0,), (0,)), ((), ())), preferred_element_type=F32
            ).astype(BF16)
            y_ref[1, rows, win] += lax.dot_general(
                sg, kk, (((0,), (0,)), ((), ())), preferred_element_type=F32
            ).astype(BF16)
            y_ref[2, rows, win] += jnp.dot(
                beside(sg), both(q), preferred_element_type=F32
            ).astype(BF16)
            y_ref[3, rows, win] += jnp.dot(
                beside(low), both(u), preferred_element_type=F32
            ).astype(BF16)
    att = y_ref[0]
    kept_ref[...] = att
    going.append(pltpu.make_async_copy(kept_ref, att_ref, kept_sem.at[1]))
    going[-1].start()
    y_ref[0] = jnp.dot(att, w_ref[...], preferred_element_type=F32).astype(BF16)
    for b in range(4):
        t = jnp.concatenate(
            [y_ref[a, pl.ds(p * 128 + b * 32, 32), :] for a in range(4) for p in range(2)], axis=0
        )
        out_ref[b] = move(back_ref[...], t).reshape(16, 16, D)
        going.append(pltpu.make_async_copy(out_ref.at[b], s_ref.at[pl.ds(b * 16, 16)], out_sem.at[b]))
        going[-1].start()
    for copy in going:
        copy.wait()


def attend(received, weight):
    order = order_to_patches(2)
    return pl.pallas_call(
        attend_kernel,
        in_specs=in_vmem(2) + in_hbm(1) + in_vmem(1),
        out_specs=in_hbm(3),
        out_shape=[
            jax.ShapeDtypeStruct((64, 16, D), BF16),
            jax.ShapeDtypeStruct((256, D), BF16),
            jax.ShapeDtypeStruct((256, D), BF16),
        ],
        scratch_shapes=[
            pltpu.VMEM((4, 16, 16, D), BF16),
            pltpu.VMEM((4, 256, D), BF16),
            pltpu.VMEM((256, D), BF16),
            pltpu.VMEM((4, 256, D), BF16),
            pltpu.VMEM((4, 16, 16, D), BF16),
            pltpu.VMEM((256, D), BF16),
            pltpu.SemaphoreType.DMA((4,)),
            pltpu.SemaphoreType.DMA((4,)),
            pltpu.SemaphoreType.DMA((2,)),
        ],
        compiler_params=params(58),
        cost_estimate=pl.CostEstimate(
            flops=6_000_000_000, bytes_accessed=20 * 256 * D + 2 * D * D, transcendentals=524288
        ),
        name="attend",
    )(const(order), const(order.T.copy()), received, weight)


def unpack_kernel(part, order_ref, slabs_ref, *refs):
    outs = refs[-8:-4]
    in_ref, rows_ref, in_sem, out_sem = refs[-4:]
    coming, going = [], []
    for g in range(4):
        coming.append(
            pltpu.make_async_copy(slabs_ref.at[pl.ds(g * 16, 16)], in_ref.at[g], in_sem.at[g])
        )
        coming[-1].start()
    for g in range(4):
        coming[g].wait()
        t = move(order_ref[...], in_ref[g].reshape(256, D))
        for a in range(4):
            for f in range(2):
                at = (a * 2 + f) * 32
                rows_ref[g, a, f] = t[at : at + 32]
            going.append(
                pltpu.make_async_copy(
                    rows_ref.at[g, a],
                    outs[a].at[0, :, pl.ds(part * 128 + g * 32, 32), :],
                    out_sem.at[g, a],
                )
            )
            going[-1].start()
    for copy in going:
        copy.wait()


def unpack(part, slabs, before):
    return pl.pallas_call(
        functools.partial(unpack_kernel, part),
        in_specs=in_vmem(1) + in_hbm(1 + len(before)),
        out_specs=in_hbm(4),
        out_shape=[jax.ShapeDtypeStruct((1, 2, 256, D), BF16)] * 4,
        scratch_shapes=[
            pltpu.VMEM((4, 16, 16, D), BF16),
            pltpu.VMEM((4, 4, 2, 32, D), BF16),
            pltpu.SemaphoreType.DMA((4,)),
            pltpu.SemaphoreType.DMA((4, 4)),
        ],
        input_output_aliases={2 + a: a for a in range(len(before))},
        compiler_params=params(60),
        cost_estimate=pl.CostEstimate(
            flops=2 * 1024 * 256 * D, bytes_accessed=4096 * D, transcendentals=0
        ),
        name="unpack",
    )(const(order_to_slabs(2).T.copy()), slabs, *before)


def outer_kernel(turn_ref, att0_ref, att1_ref, cot0_ref, cot1_ref, mine_ref, theirs_ref):
    att = jnp.concatenate([att0_ref[...], att1_ref[...]], axis=0)
    cot = jnp.concatenate([cot0_ref[...], cot1_ref[...]], axis=0)
    turned = move(cot, turn_ref[...])
    parts = [att[:, 288 * b : 288 * b + 288] for b in range(4)]
    core = lax.axis_index("c")

    def product(left, even, odd):
        chosen = jnp.where(core == 0, even, odd)
        return lax.dot_general(left, chosen, (((0,), (0,)), ((), ())), preferred_element_type=F32)

    theirs_ref[:, :288] = product(cot, parts[1], parts[0]).astype(BF16)
    theirs_ref[:, 288:] = product(turned, parts[3], parts[2]).astype(BF16)
    mine_ref[:, :288] = product(cot, parts[0], parts[1])
    mine_ref[:, 288:] = product(turned, parts[2], parts[3])


def turn():
    order = np.arange(D).reshape(4, 4, 4, 18).transpose(2, 0, 1, 3).reshape(-1)
    out = np.zeros((D, D), np.float32)
    out[order, np.arange(D)] = 1
    return const(out)


def outer(atts, cots):
    return pl.pallas_call(
        outer_kernel,
        in_specs=in_vmem(5),
        out_specs=in_vmem(2),
        out_shape=[jax.ShapeDtypeStruct((D, 576), F32), jax.ShapeDtypeStruct((D, 576), BF16)],
        compiler_params=params(24),
        cost_estimate=pl.CostEstimate(
            flops=2 * 512 * D * D, bytes_accessed=4 * 512 * D + 6 * D * 576, transcendentals=0
        ),
        name="outer",
    )(turn(), *atts, *cots)


def halves_kernel(mine_ref, other_ref, own_ref, *out_refs):
    for i, axis in enumerate(("y", "x")):
        columns = slice(288 * i, 288 * i + 288)
        at = lax.axis_index(axis)
        for k in range(4):
            rows = pl.ds(pl.multiple_of((at ^ k) * 288, 32), 288)
            total = mine_ref[rows, columns] + other_ref[rows, columns].astype(F32)
            if k == 0:
                own_ref[i] = total
            else:
                out_refs[3 * i + k - 1][...] = total.astype(BF16)


def halves(mine, other):
    return pl.pallas_call(
        halves_kernel,
        in_specs=in_vmem(2),
        out_specs=in_vmem(7),
        out_shape=[jax.ShapeDtypeStruct((2, 288, 288), F32)] + [jax.ShapeDtypeStruct((288, 288), BF16)] * 6,
        compiler_params=params(24),
        cost_estimate=pl.CostEstimate(flops=D * 576, bytes_accessed=10 * D * 576, transcendentals=0),
        name="halves",
    )(mine, other)


SIZES = {"y": 4, "x": 4, "zl": 4, "zh": 2, "c": 2, ("zl", "zh"): 8}


def swap(value, axis, k):
    return lax.ppermute(value, axis, [(i, i ^ k) for i in range(SIZES[axis])])


def terms_over(blocks, axis):
    at = lax.axis_index(axis)
    own = lax.dynamic_index_in_dim(blocks, at, 0, keepdims=False)
    return [own] + [
        swap(lax.dynamic_index_in_dim(blocks, at ^ k, 0, keepdims=False), axis, k)
        for k in range(1, SIZES[axis])
    ]


def weight_terms(atts, cots):
    mine, theirs = outer(atts, cots)
    own, *sent = halves(mine, swap(theirs, "c", 1))
    here, there = own[0], own[1]
    for k in range(1, 4):
        here = here + swap(sent[k - 1], "y", k).astype(F32)
        there = there + swap(sent[k + 2], "x", k).astype(F32)
    first = [here, there]
    here = sum(terms_over(here.reshape(4, 4, 18, 288).transpose(1, 0, 2, 3).reshape(4, 72, 288), "x"))
    there = sum(terms_over(there.reshape(4, 72, 288), "y"))
    return first, terms_over(jnp.stack([t.reshape(4, 18, 288) for t in (here, there)], axis=1).reshape(8, 18, 288), ("zl", "zh"))


def by_rank(axis, own, other):
    first = lax.axis_index(axis) == 0
    return jnp.stack([jnp.where(first, own, other), jnp.where(first, other, own)])


def whole_weight(piece, other):
    pair = by_rank("zh", piece, other)
    rows = lax.all_gather(pair, ("y", "x"), axis=0, tiled=False)
    rows = rows.transpose(1, 0, 2, 3).reshape(2, 288, D)
    both = by_rank("c", rows, swap(rows, "c", 1))
    return both.transpose(1, 0, 2, 3).reshape(D, D)


def hold_kernel(*refs):
    pass


def hold(value, tokens):
    return pl.pallas_call(
        hold_kernel,
        in_specs=[pl.BlockSpec(memory_space=pl.ANY)] * (1 + len(tokens)),
        out_specs=pl.BlockSpec(memory_space=pl.ANY),
        out_shape=jax.ShapeDtypeStruct(value.shape, value.dtype),
        input_output_aliases={0: 0},
        name="hold",
    )(value, *tokens)


def exchange(t):
    return lax.all_to_all(t, SEQ, split_axis=0, concat_axis=0, tiled=True)


def on_device(queries, keys, values, cotangent, out_weight):
    arrays = (queries, keys, values, cotangent)
    place = lax.axis_index("y") * 4 + lax.axis_index("x")
    piece = lax.dynamic_slice_in_dim(out_weight, place * 18, 18, 0)
    other = swap(piece, "zh", 1)
    received = [exchange(hold(pack(0, arrays, []), [other])), exchange(pack(1, arrays, []))]
    weight = whole_weight(piece, other)
    sent, atts, cots = zip(*[attend(t, weight) for t in received])
    begun, terms = weight_terms(atts, cots)
    outs = unpack(0, exchange(sent[0]), ())
    outs = unpack(1, exchange(hold(sent[1], begun)), outs)
    return (*outs, sum(terms).T)


def solution(mesh):
    fine = Mesh(mesh.devices.reshape(4, 4, 4, 2, 2), ("y", "zl", "x", "zh", "c"))
    frames = P(ROWS, SEQ, None, None)
    return jax.shard_map(
        on_device,
        mesh=fine,
        in_specs=(frames, frames, frames, frames, P(ROWS, None)),
        out_specs=(frames, frames, frames, frames, P(ROWS, SEQ)),
        check_vma=False,
    )
```
